256 devices in a mesh: gx: 16 (over z_hi, x), gy: 16 (over z_lo, y, core).
Axes of the slice: x: 4, y: 4, z: 8 (z_hi: 4, z_lo: 2; z = z_hi * 2 + z_lo), core: 2. Of those that a mesh axis runs over, the one named last changes fastest.
Arguments:
- facies: int32 [128, 256, 128], P('gx', 'gy'), may hold values from 0 to 7
- source: float32 [128, 256, 128], P('gx', 'gy'), may hold values from -5 to 5
- facies_perm: float32 [8], replicated, may hold values from 0.5 to 5
- facies_store: float32 [8], replicated, may hold values from 0.0002 to 0.001
- well_x: int32 [64], replicated, may hold values from 0 to 127
- well_y: int32 [64], replicated, may hold values from 0 to 255
- well_rate: float32 [64], replicated, may hold values from -2000 to 2000
Outputs:
- pressure: float32 [128, 256, 128], P('gx', 'gy')
The draws below stay inside these ranges and needn't reach their ends.
All inputs are finite; a program needn't handle non-finite values.
Results may differ from the reference program's by a relative error of at most 0.0003.
Values sent between devices are 32-bit elements; how exact they have to be, the bound alone decides.
A program may use at most 128 MiB of HBM per device.

```python
import math
import jax
import jax.numpy as jnp
import numpy as np
from jax import lax

CELLS_Z = 128
BLOCK_X = 64
BLOCK_Y = 64
BLOCK_Z = 16
SWEEPS = 3
FACIES = 8
WELL_COUNT = 64
GRID_X = 128
GRID_Y = 256
BLOCKS_X = 2
BLOCKS_Y = 4
BLOCKS_Z = 8
COARSE = 64
SEGMENTS = 9


def draw_source(key, part):
    rough_part = jnp.clip(jax.random.normal(key, (GRID_X, GRID_Y, CELLS_Z), jnp.float32), -4.0, 4.0)
    layer_pos = (jnp.arange(CELLS_Z, dtype=jnp.float32) + 0.5) / BLOCK_Z
    layered = jnp.sin(3.14159265 * layer_pos)
    return rough_part + 0.5 * layered[None, None, :]


def place_ends(entries, stream_key, low, high):
    spot = [jax.random.randint(jax.random.fold_in(stream_key, axis), (), 0, length) for axis, length in enumerate(entries.shape)]
    longest = entries.shape.index(max(entries.shape))
    neighbour = spot[:longest] + [(spot[longest] + 1) % entries.shape[longest]] + spot[longest + 1:]
    return entries.at[tuple(spot)].set(low).at[tuple(neighbour)].set(high)


def setup_inputs(seed: int = 0) -> dict:
    streams_of = jax.random.split(jax.random.key(seed), 8)
    facies = place_ends(jax.random.randint(streams_of[0], (GRID_X, GRID_Y, CELLS_Z), 0, FACIES), jax.random.fold_in(streams_of[0], 1), 0, FACIES - 1).astype(jnp.int32)
    source = draw_source(jax.random.fold_in(streams_of[7], 71), 0)
    facies_perm = jnp.clip(jnp.exp(jax.random.uniform(streams_of[2], (FACIES,), jnp.float32, math.log(0.5), math.log(5.0))), 0.5, 5.0)
    facies_store = jnp.clip(jnp.exp(jax.random.uniform(streams_of[3], (FACIES,), jnp.float32, math.log(0.0002), math.log(0.001))), 0.0002, 0.001)
    well_x = place_ends(jax.random.randint(streams_of[4], (WELL_COUNT,), 0, GRID_X), jax.random.fold_in(streams_of[4], 1), 0, GRID_X - 1).astype(jnp.int32)
    well_y = place_ends(jax.random.randint(streams_of[5], (WELL_COUNT,), 0, GRID_Y), jax.random.fold_in(streams_of[5], 1), 0, GRID_Y - 1).astype(jnp.int32)
    well_rate = jnp.clip(jax.random.uniform(streams_of[6], (WELL_COUNT,), jnp.float32, -2000.0, 2000.0), -2000.0, 2000.0)
    return dict(facies=facies, source=source, facies_perm=facies_perm, facies_store=facies_store, well_x=well_x, well_y=well_y, well_rate=well_rate)


RELAX_WEIGHT = 2.0 / 3.0
HIGHEST = lax.Precision.HIGHEST
first_bits = np.array([0, 0, 0, 0, 1, 1, 1, 1], dtype=np.int32)
second_bits = np.array([0, 0, 1, 1, 0, 0, 1, 1], dtype=np.int32)
third_bits = np.array([0, 1, 0, 1, 0, 1, 0, 1], dtype=np.int32)
shift_along_x = np.array([0, 2, -2, 0, 0, 0, 0], dtype=np.int32)
shift_along_y = np.array([0, 0, 0, 2, -2, 0, 0], dtype=np.int32)
shift_along_z = np.array([0, 0, 0, 0, 0, 2, -2], dtype=np.int32)

def support_of(coords, block_size, parity):
    return (parity + 2 * jnp.floor_divide(coords + block_size // 2 - block_size * parity, 2 * block_size)).astype(jnp.int32)

def parity_nodes(coords, block_size):
    return jnp.stack([support_of(coords, block_size, 0), support_of(coords, block_size, 1)])

def parity_start(coords, block_size):
    node_ids = parity_nodes(coords, block_size)
    return (node_ids == jnp.floor_divide(coords, block_size)[None]).astype(jnp.float32)

def parity_same(coords, block_size):
    node_here = parity_nodes(coords[:-1], block_size)
    node_next = parity_nodes(coords[1:], block_size)
    return (node_here == node_next).astype(jnp.float32)

def harmonic(left_perm, right_perm):
    return 2.0 * left_perm * right_perm / (left_perm + right_perm)

def face_pad(values_in, dim_id, before):
    widths = [(0, 0), (0, 0), (0, 0)]
    widths[dim_id] = (1, 0) if before else (0, 1)
    return jnp.pad(values_in, widths)

def expand(line_in, dim_id):
    new_shape = [1, 1, 1]
    new_shape[dim_id] = line_in.shape[0]
    return line_in.reshape(new_shape)

def split_faces(values_in, dim_id):
    length = values_in.shape[dim_id]
    below_part = lax.slice_in_dim(values_in, 0, length - 1, axis=dim_id)
    above_part = lax.slice_in_dim(values_in, 1, length, axis=dim_id)
    return (below_part, above_part)

def cut_apply(values_in, storage, trans_all, same_all):
    result = storage * values_in
    for dim_id in range(3):
        trans_face = trans_all[dim_id]
        same_line = expand(same_all[dim_id], dim_id)
        below_part, above_part = split_faces(values_in, dim_id)
        result = result + face_pad(trans_face * (below_part - same_line * above_part), dim_id, False)
        result = result + face_pad(trans_face * (above_part - same_line * below_part), dim_id, True)
    return result

def rim_terms(values_in, trans_all, same_all):
    result = []
    for dim_id in range(3):
        trans_face = trans_all[dim_id]
        cross_mask = 1.0 - expand(same_all[dim_id], dim_id)
        below_part, above_part = split_faces(values_in, dim_id)
        result.append(face_pad(-trans_face * cross_mask * above_part, dim_id, False))
        result.append(face_pad(-trans_face * cross_mask * below_part, dim_id, True))
    return result

def diagonal_of(storage, trans_all):
    result = storage
    for dim_id in range(3):
        result = result + face_pad(trans_all[dim_id], dim_id, False) + face_pad(trans_all[dim_id], dim_id, True)
    return result

def lookup(facies, code_table):
    result = jnp.zeros(facies.shape, jnp.float32)
    for code_id in range(code_table.shape[0]):
        result = result + jnp.where(facies == code_id, code_table[code_id], 0.0)
    return result

def flatten_node(index_x, index_y, index_z, counts):
    count_x, count_y, count_z = counts
    flat_ids = (jnp.clip(index_x, 0, count_x - 1) * count_y + jnp.clip(index_y, 0, count_y - 1)) * count_z
    return (flat_ids + jnp.clip(index_z, 0, count_z - 1)).astype(jnp.int32)

def tile_indices(anchor_x, anchor_y, counts, layers):
    count_x, count_y, count_z = counts
    row_x = parity_nodes(jnp.reshape(anchor_x, (1,)).astype(jnp.int32), BLOCK_X)[first_bits][:, 0]
    row_y = parity_nodes(jnp.reshape(anchor_y, (1,)).astype(jnp.int32), BLOCK_Y)[second_bits][:, 0]
    seg_first = jnp.maximum(jnp.arange(count_z + 1, dtype=jnp.int32) * BLOCK_Z - BLOCK_Z // 2, 0).astype(jnp.int32)
    row_z = parity_nodes(seg_first, BLOCK_Z)[third_bits]
    row_ids = flatten_node(row_x[:, None], row_y[:, None], row_z, counts)
    col_ids = flatten_node(row_x[:, None, None] + jnp.asarray(shift_along_x)[None, :, None], row_y[:, None, None] + jnp.asarray(shift_along_y)[None, :, None], row_z[:, None, :] + jnp.asarray(shift_along_z)[None, :, None], counts)
    entry_ids = (row_ids[None, :, None, :] * (count_x * count_y * count_z) + col_ids[:, None, :, :]).astype(jnp.int32)
    return (entry_ids, row_ids)

def segment_matrix(layers, segment_count):
    seg_of = (jnp.arange(layers, dtype=jnp.int32) + BLOCK_Z // 2) // BLOCK_Z
    return (seg_of[:, None] == jnp.arange(segment_count, dtype=jnp.int32)[None, :]).astype(jnp.float32)

def solve_coarse(coarse, coarse_rhs):
    factor = jnp.linalg.cholesky(coarse)
    middle = lax.linalg.triangular_solve(factor, coarse_rhs[:, None], left_side=True, lower=True)
    return lax.linalg.triangular_solve(factor, middle, left_side=True, lower=True, transpose_a=True)[:, 0]

def reference(facies, source, facies_perm, facies_store, well_x, well_y, well_rate):
    perm_cell = lookup(facies, facies_perm)
    storage = lookup(facies, facies_store)
    trans_all = tuple((harmonic(*split_faces(perm_cell, dim_id)) for dim_id in range(3)))
    diagonal = diagonal_of(storage, trans_all)
    coord_x = jnp.arange(GRID_X, dtype=jnp.int32)
    coord_y = jnp.arange(GRID_Y, dtype=jnp.int32)
    coord_z = jnp.arange(CELLS_Z, dtype=jnp.int32)
    start_x = parity_start(coord_x, BLOCK_X)[first_bits]
    start_y = parity_start(coord_y, BLOCK_Y)[second_bits]
    start_z = parity_start(coord_z, BLOCK_Z)[third_bits]
    basis_now = start_x[:, :, None, None] * start_y[:, None, :, None] * start_z[:, None, None, :]
    same_x8 = parity_same(coord_x, BLOCK_X)[first_bits]
    same_y8 = parity_same(coord_y, BLOCK_Y)[second_bits]
    same_z8 = parity_same(coord_z, BLOCK_Z)[third_bits]

    def change_of(item_set):
        return -RELAX_WEIGHT * cut_apply(item_set[0], storage, trans_all, (item_set[1], item_set[2], item_set[3])) / diagonal
    for sweep_id in range(SWEEPS):
        changes = lax.map(change_of, (basis_now, same_x8, same_y8, same_z8))
        change_sum = jnp.sum(changes, axis=0)
        basis_now = basis_now + changes - basis_now * change_sum[None]
    hit_x = (well_x[:, None] == coord_x[None, :]).astype(jnp.float32)
    hit_y = (well_y[:, None] == coord_y[None, :]).astype(jnp.float32)
    column = jnp.einsum('w,wx,wy->xy', well_rate, hit_x, hit_y, precision=HIGHEST)
    rhs_fine = source + column[:, :, None] / CELLS_Z
    half_x = BLOCK_X // 2
    half_y = BLOCK_Y // 2
    tiles_x = GRID_X // half_x
    tiles_y = GRID_Y // half_y
    zmatrix = segment_matrix(CELLS_Z, SEGMENTS)
    shaped = basis_now.reshape(8, tiles_x, half_x, tiles_y, half_y, CELLS_Z)

    def gram_of(item_set):
        same_three = (item_set[1], item_set[2], item_set[3])
        term_list = [cut_apply(item_set[0], storage, trans_all, same_three)] + rim_terms(item_set[0], trans_all, same_three)
        term_stack = jnp.stack(term_list).reshape(7, tiles_x, half_x, tiles_y, half_y, CELLS_Z)
        gram_tile = jnp.einsum('aipjqz,sipjqz->ijasz', shaped, term_stack, precision=HIGHEST)
        return jnp.einsum('ijasz,zg->ijasg', gram_tile, zmatrix, precision=HIGHEST)
    grams = lax.map(gram_of, (basis_now, same_x8, same_y8, same_z8))
    grams = jnp.transpose(grams, (1, 2, 0, 3, 4, 5))
    counts = (BLOCKS_X, BLOCKS_Y, BLOCKS_Z)

    def indices_for(first_x, first_y):
        return tile_indices(first_x, first_y, counts, CELLS_Z)
    anchors_x = jnp.arange(tiles_x, dtype=jnp.int32) * half_x
    anchors_y = jnp.arange(tiles_y, dtype=jnp.int32) * half_y
    entry_ids, row_ids = jax.vmap(jax.vmap(indices_for, in_axes=(None, 0)), in_axes=(0, None))(anchors_x, anchors_y)
    coarse = jnp.zeros((COARSE * COARSE,), jnp.float32).at[entry_ids.reshape(-1)].add(grams.reshape(-1)).reshape(COARSE, COARSE)
    rhs_tile = jnp.einsum('aipjqz,ipjqz->ijaz', shaped, rhs_fine.reshape(tiles_x, half_x, tiles_y, half_y, CELLS_Z), precision=HIGHEST)
    rhs_tile = jnp.einsum('ijaz,zg->ijag', rhs_tile, zmatrix, precision=HIGHEST)
    coarse_rhs = jnp.zeros((COARSE,), jnp.float32).at[row_ids.reshape(-1)].add(rhs_tile.reshape(-1))
    coarse_solution = solve_coarse(coarse, coarse_rhs)
    values_at = coarse_solution[row_ids]
    per_layer = jnp.einsum('ijag,zg->ijaz', values_at, zmatrix, precision=HIGHEST)
    prolonged = jnp.einsum('aipjqz,ijaz->ipjqz', shaped, per_layer, precision=HIGHEST).reshape(GRID_X, GRID_Y, CELLS_Z)
    ones_all = (jnp.ones((GRID_X - 1,), jnp.float32), jnp.ones((GRID_Y - 1,), jnp.float32), jnp.ones((CELLS_Z - 1,), jnp.float32))
    applied = cut_apply(prolonged, storage, trans_all, ones_all)
    return prolonged + RELAX_WEIGHT * (rhs_fine - applied) / diagonal
```

```python
import functools

import jax
import jax.numpy as jnp
from jax import lax
from jax.experimental import pallas as pl
from jax.experimental.pallas import tpu as pltpu
from jax.sharding import PartitionSpec as P

GRID_X, GRID_Y, CELLS_Z = 128, 256, 128
BLOCK_X, BLOCK_Y, BLOCK_Z = 64, 64, 16
FACIES = 8
WELLS = 64
RELAX = 2.0 / 3.0

TX, TY = 8, 16
HX, HY = 4, 8
EX, EY = TX + 2 * HX, TY + 2 * HY
DX, DY = 16, 16
MESH = pl.DeviceIdType.MESH
F32 = jnp.float32

COLORS = [(c >> 2 & 1, c >> 1 & 1, c & 1) for c in range(8)]
SLOT = [4 * i + j + 8 * k for i, j, k in COLORS]
RHS_SLOT = 2


def roll(value, shift):
    return pltpu.roll(value, shift % 128, 1)


def iota(dim):
    return lax.broadcasted_iota(jnp.int32, (8, 128), dim)


def flag(cond):
    return jnp.where(cond, 1.0, 0.0).astype(F32)


def same_xy(coord, parity, block):
    return flag((coord + 1 + block // 2 - block * parity + 4 * block) % (2 * block) != 0)


def same_z(coord, parity):
    return flag((coord + 1 + BLOCK_Z // 2 - BLOCK_Z * parity + 2 * BLOCK_Z) % (2 * BLOCK_Z) != 0)


def inside(coord, total):
    return (coord >= 0) & (coord < total)


def kernel(
    facies_ref, source_ref, perm_ref, store_ref, wx_ref, wy_ref, wr_ref, out_ref,
    fac, hperm, stor, coef, trans, wdiag, va, vb, bv, rhs, wide, stage1, stage2, val, prol,
    mine, half, hsend, hrecv, xsend, xrecv, ysend, yrecv,
):
    gx = lax.axis_index("gx")
    gy = lax.axis_index("gy")
    ax, ay = gx * TX, gy * TY
    lane, sub = iota(1), iota(0)

    barrier = pltpu.get_barrier_semaphore()
    partners = [((gx + d) % DX, gy) for d in range(1, DX)]
    partners += [(gx, (gy + d) % DY) for d in range(1, DY)]
    corners = [((gx + i) % DX, (gy + j) % DY) for i in (1, DX - 1) for j in (1, DY - 1)]
    for who in partners + corners:
        pl.semaphore_signal(barrier, inc=1, device_id=who, device_id_type=MESH)
    pl.semaphore_wait(barrier, len(partners) + 4)

    copies = []
    n = 0
    for dx in (-1, 0, 1):
        for dy in (-1, 0, 1):
            if dx == 0 and dy == 0:
                continue
            sx = {1: (TX - HX, HX), -1: (0, HX), 0: (0, TX)}[dx]
            sy = {1: (TY - HY, HY), -1: (0, HY), 0: (0, TY)}[dy]
            tx = {1: 0, -1: HX + TX, 0: HX}[dx]
            ty = {1: 0, -1: HY + TY, 0: HY}[dy]
            copies.append(
                pltpu.make_async_remote_copy(
                    src_ref=facies_ref.at[pl.ds(sx[0], sx[1]), pl.ds(sy[0], sy[1])],
                    dst_ref=fac.at[pl.ds(tx, sx[1]), pl.ds(ty, sy[1])],
                    send_sem=hsend.at[n],
                    recv_sem=hrecv.at[n],
                    device_id=((gx + dx + DX) % DX, (gy + dy + DY) % DY),
                    device_id_type=MESH,
                )
            )
            n += 1
    for copy in copies:
        copy.start()

    well_x = wx_ref[...]
    well_y = wy_ref[...]
    well_r = wr_ref[...]
    sub64 = lax.broadcasted_iota(jnp.int32, (8, WELLS), 0)
    for j in range(2):
        hit_y = jnp.where(sub64 + (ay + 8 * j) == well_y, well_r, 0.0)
        for x in range(TX):
            part = jnp.where(well_x == ax + x, hit_y, 0.0)
            column = jnp.sum(part, axis=1, keepdims=True)
            rhs[x, 8 * j : 8 * j + 8, :] = source_ref[x, 8 * j : 8 * j + 8, :] + column / CELLS_Z

    def start_plane(x, _):
        gxe = ax - HX + x
        for t in range(4):
            row = ay - HY + 8 * t + sub
            for c, (i, j, k) in enumerate(COLORS):
                hit = inside(row, GRID_Y) & ((row // BLOCK_Y) % 2 == j) & ((lane // BLOCK_Z) % 2 == k)
                hitx = inside(gxe, GRID_X) & ((gxe + 2 * BLOCK_X) // BLOCK_X % 2 == i)
                va[c, x, 8 * t : 8 * t + 8, :] = flag(hit) * flag(hitx)
        return 0

    lax.fori_loop(0, EX, start_plane, 0)

    fac[HX : HX + TX, HY : HY + TY, :] = facies_ref[...]
    for copy in copies:
        copy.wait()

    half_inv = [0.5 / jnp.full((8, 128), perm_ref[f], F32) for f in range(FACIES)]
    store_at = [jnp.full((8, 128), store_ref[f], F32) for f in range(FACIES)]

    def pick(code, table):
        bits = [(code // (1 << b)) % 2 == 1 for b in range(3)]
        for b in range(3):
            table = [jnp.where(bits[b], hi, lo) for lo, hi in zip(table[::2], table[1::2])]
        return table[0]

    def lookup_plane(x, _):
        for t in range(4):
            code = fac[x, 8 * t : 8 * t + 8, :]
            hperm[x, 8 * t : 8 * t + 8, :] = pick(code, half_inv)
            stor[x, 8 * t : 8 * t + 8, :] = pick(code, store_at)
        return 0

    lax.fori_loop(0, EX, lookup_plane, 0)

    last_z = flag(lane < CELLS_Z - 1)

    def coef_plane(x, _):
        gxe = ax - HX + x
        ok_m = flag(inside(gxe - 1, GRID_X) & inside(gxe, GRID_X))
        ok_p = flag(inside(gxe, GRID_X) & inside(gxe + 1, GRID_X))
        for t in range(3):
            r = 4 + 8 * t
            h = hperm[x, r : r + 8, :]
            row = ay - HY + r + sub
            row_m = flag(inside(row - 1, GRID_Y) & inside(row, GRID_Y))
            row_p = flag(inside(row, GRID_Y) & inside(row + 1, GRID_Y))
            txm = ok_m / (h + hperm[x - 1, r : r + 8, :])
            txp = ok_p / (h + hperm[x + 1, r : r + 8, :])
            tym = row_m / (h + hperm[x, r - 1 : r + 7, :])
            typ = row_p / (h + hperm[x, r + 1 : r + 9, :])
            tzp = last_z / (h + roll(h, -1))
            tzm = roll(tzp, 1)
            diag = stor[x, r : r + 8, :] + txm + txp + tym + typ + tzm + tzp
            w = RELAX / diag
            wdiag[x, r : r + 8, :] = w
            for n, value in enumerate((txm, txp, tym, typ, tzm, tzp)):
                trans[n, x, r : r + 8, :] = value
            wxm, wxp, wym, wyp, wzm, wzp = [w * v for v in (txm, txp, tym, typ, tzm, tzp)]
            a = 8 * t
            for p in range(2):
                coef[p, x, a : a + 8, :] = wxm * same_xy(gxe - 1, p, BLOCK_X)
                coef[2 + p, x, a : a + 8, :] = wxp * same_xy(gxe, p, BLOCK_X)
                coef[4 + p, x, a : a + 8, :] = wym * same_xy(row - 1, p, BLOCK_Y)
                coef[6 + p, x, a : a + 8, :] = wyp * same_xy(row, p, BLOCK_Y)
                coef[8 + p, x, a : a + 8, :] = wzm * same_z(lane - 1, p)
                coef[10 + p, x, a : a + 8, :] = wzp * same_z(lane, p)
        return 0

    lax.fori_loop(1, EX - 1, coef_plane, 0)

    def sweep(src, dst, low):
        def plane(x, _):
            for t in range(3):
                r, a = 4 + 8 * t, 8 * t
                k = [coef[n, x, a : a + 8, :] for n in range(12)]
                old, new = [], []
                for c, (px, py, pz) in enumerate(COLORS):
                    v = src[c, x, r : r + 8, :]
                    q = k[px] * src[c, x - 1, r : r + 8, :] + k[2 + px] * src[c, x + 1, r : r + 8, :]
                    q += k[4 + py] * src[c, x, r - 1 : r + 7, :] + k[6 + py] * src[c, x, r + 1 : r + 9, :]
                    q += k[8 + pz] * roll(v, 1) + k[10 + pz] * roll(v, -1)
                    old.append(v)
                    new.append(q)
                total = functools.reduce(jnp.add, new) - RELAX * functools.reduce(jnp.add, old)
                keep = (1.0 - RELAX) - total
                for c in range(8):
                    dst[c, x, r : r + 8, :] = new[c] + old[c] * keep
            return 0

        lax.fori_loop(low, EX - low, plane, 0)

    sweep(va, vb, 1)
    sweep(vb, va, 2)
    sweep(va, vb, 3)
    basis = vb

    def apply_plane(x, _):
        for t in range(2):
            r = HY + 8 * t
            row = ay + 8 * t + sub
            k = [trans[n, x, r : r + 8, :] for n in range(6)]
            s = stor[x, r : r + 8, :]
            ym = [same_xy(row - 1, p, BLOCK_Y) for p in range(2)]
            yp = [same_xy(row, p, BLOCK_Y) for p in range(2)]
            zm = [same_z(lane - 1, p) for p in range(2)]
            zp = [same_z(lane, p) for p in range(2)]
            for c, (px, py, pz) in enumerate(COLORS):
                v = basis[c, x, r : r + 8, :]
                q = s * v
                q += k[0] * (v - basis[c, x - 1, r : r + 8, :]) + k[1] * (v - basis[c, x + 1, r : r + 8, :])
                q += k[2] * (v - ym[py] * basis[c, x, r - 1 : r + 7, :])
                q += k[3] * (v - yp[py] * basis[c, x, r + 1 : r + 9, :])
                q += k[4] * (v - zm[pz] * roll(v, 1)) + k[5] * (v - zp[pz] * roll(v, -1))
                bv[c, x - HX, 8 * t : 8 * t + 8, :] = q
        return 0

    lax.fori_loop(HX, HX + TX, apply_plane, 0)

    pairs = [(a, c) for a in range(8) for c in range(a, 8)]
    for group in (pairs[:15], pairs[15:30], pairs[30:]):
        rows = sorted({a for a, _ in group})
        cols = sorted({c for _, c in group})
        last = group is not None and group[-1] == (7, 7)

        def gather(x, acc, group=group, rows=rows, cols=cols, last=last):
            acc = list(acc)
            for t in range(2):
                left = {a: basis[a, x + HX, HY + 8 * t : HY + 8 * t + 8, :] for a in (range(8) if last else rows)}
                right = {c: bv[c, x, 8 * t : 8 * t + 8, :] for c in cols}
                for n, (a, c) in enumerate(group):
                    acc[n] = acc[n] + left[a] * right[c]
                if last:
                    load = rhs[x, 8 * t : 8 * t + 8, :]
                    for a in range(8):
                        acc[len(group) + a] = acc[len(group) + a] + left[a] * load
            return tuple(acc)

        count = len(group) + (8 if last else 0)
        acc = lax.fori_loop(0, TX, gather, tuple(jnp.zeros((8, 128), F32) for _ in range(count)))
        for n, (a, c) in enumerate(group):
            line = jnp.sum(acc[n], axis=0, keepdims=True)
            wide[c, a : a + 1, :] = line
            if a != c:
                wide[a, c : c + 1, :] = line
        if last:
            for a in range(8):
                wide[8, a : a + 1, :] = jnp.sum(acc[len(group) + a], axis=0, keepdims=True)

    packed = jnp.zeros((8, 128), F32)
    for n in range(9):
        line = wide[n]
        for step in (1, 2, 4, 8):
            line = line + roll(line, -step)
        line = jnp.where(lane % 16 == 8, line, 0.0)
        packed = packed + roll(line, 8 + (SLOT[n] if n < 8 else RHS_SLOT))

    def exchange(src, slots, send, recv, axis):
        me = gx if axis == 0 else gy
        size = DX if axis == 0 else DY
        sent = []
        for d in range(1, size):
            to = ((gx + d) % DX, gy) if axis == 0 else (gx, (gy + d) % DY)
            copy = pltpu.make_async_remote_copy(
                src_ref=src, dst_ref=slots.at[me], send_sem=send.at[d], recv_sem=recv.at[d],
                device_id=to, device_id_type=MESH,
            )
            copy.start()
            sent.append(copy)
        slots[me] = src[...]
        for copy in sent:
            copy.wait()

    def tree(items):
        while len(items) > 1:
            items = [a + b for a, b in zip(items[::2], items[1::2])] + (items[-1:] if len(items) % 2 else [])
        return items[0]

    mine[...] = packed
    exchange(mine, stage1, xsend, xrecv, 0)
    half[...] = tree([stage1[n] for n in range(DX)])
    exchange(half, stage2, ysend, yrecv, 1)
    sa = tree([stage2[n] for n in range(0, 6)])
    sb = tree([stage2[n] for n in range(6, 10)])
    sc = tree([stage2[n] for n in range(10, 16)])

    pair_j = lane % 4
    low = pair_j < 2
    zero = jnp.zeros((8, 128), F32)

    def put(j0=zero, j1=zero, j2=zero, j3=zero):
        first = jnp.where(pair_j == 0, j0, jnp.where(pair_j == 1, j1, 0.0))
        second = jnp.where(pair_j == 0, j2, jnp.where(pair_j == 1, j3, 0.0))
        return first + roll(second, 2)

    line_of = [
        put(sa, sa),
        put(sa, sa + sb, sb),
        put(zero, sb, sb + sc, sc),
        put(zero, zero, sc, sc),
    ]
    load_of = [sa, sa + sb, sb + sc, sc]
    group = lane // 16
    used = lane % 16 < 8
    even = sub % 2 == 0
    on = used & (group == sub)
    above = used & (group == sub + 1)
    below = used & (group == sub - 1)
    matrix = []
    for ij in range(8):
        i, j = ij // 4, ij % 4
        e = 4 * i + 2 * (j % 2)
        base = line_of[j]
        turns = {s: roll(base, -s) for s in (8, 16, 24)}
        turns[0] = base
        be = {s: jnp.broadcast_to(v[e : e + 1, :], (8, 128)) for s, v in turns.items()}
        bo = {s: jnp.broadcast_to(v[e + 1 : e + 2, :], (8, 128)) for s, v in turns.items()}
        diag_part = jnp.where(even, be[0] + be[16], bo[8] + bo[24])
        up = jnp.where(even, be[8], bo[0])
        down = jnp.where(even, be[24], bo[16])
        block = jnp.where(on, diag_part, jnp.where(above, up, jnp.where(below, down, 0.0)))
        load = jnp.where(lane % 16 == RHS_SLOT, load_of[j], 0.0)
        load = load + roll(load, -16)
        le = jnp.broadcast_to(load[e : e + 1, :], (8, 128))
        lo = jnp.broadcast_to(load[e + 1 : e + 2, :], (8, 128))
        load = jnp.where((group == sub) & (lane % 16 == RHS_SLOT), jnp.where(even, le, lo), 0.0)
        load = jnp.sum(load, axis=1, keepdims=True)
        matrix.append(jnp.where(lane == 8, load, block))

    for kk in range(8):
        for ij in range(8):
            at = 16 * kk + ij
            columns = [m[:, at : at + 1] for m in matrix]
            row = jnp.broadcast_to(matrix[ij][kk : kk + 1, :], (8, 128))
            pivot = jnp.broadcast_to(columns[ij][kk : kk + 1, :], (8, 1))
            row = row / pivot
            for n in range(8):
                update = matrix[n] - columns[n] * row
                if n == ij:
                    update = jnp.where(sub == kk, row, update)
                matrix[n] = update

    node_k = [2 * ((lane + BLOCK_Z // 2) // (2 * BLOCK_Z)),
              2 * ((lane + BLOCK_Z // 2 + BLOCK_Z) // (2 * BLOCK_Z)) - 1]
    for ij in range(8):
        u = matrix[ij][:, 8:9]
        for p in range(2):
            line = jnp.sum(jnp.where(node_k[p] == sub, u, 0.0), axis=0, keepdims=True)
            val[p, ij : ij + 1, :] = line

    def node_row(px, py, pz, tile):
        first = tile * TY
        j = py + 2 * ((first + BLOCK_Y // 2 - BLOCK_Y * py + 4 * BLOCK_Y) // (2 * BLOCK_Y) - 2)
        j = jnp.clip(j, 0, 3)
        return val[pz, pl.ds(4 * px + j, 1), :]

    for t in range(4):
        tile = gy + (-1, 0, 0, 1)[t]
        weights = [jnp.broadcast_to(node_row(px, py, pz, tile), (8, 128)) for px, py, pz in COLORS]

        def prolong(x, _, t=t, weights=weights):
            prol[x, 8 * t : 8 * t + 8, :] = functools.reduce(
                jnp.add, [weights[c] * basis[c, x, 8 * t : 8 * t + 8, :] for c in range(8)]
            )
            return 0

        lax.fori_loop(HX - 1, HX + TX + 1, prolong, 0)

    def finish(x, _):
        for t in range(2):
            r = HY + 8 * t
            v = prol[x, r : r + 8, :]
            k = [trans[n, x, r : r + 8, :] for n in range(6)]
            q = stor[x, r : r + 8, :] * v
            q += k[0] * (v - prol[x - 1, r : r + 8, :]) + k[1] * (v - prol[x + 1, r : r + 8, :])
            q += k[2] * (v - prol[x, r - 1 : r + 7, :]) + k[3] * (v - prol[x, r + 1 : r + 9, :])
            q += k[4] * (v - roll(v, 1)) + k[5] * (v - roll(v, -1))
            load = rhs[x - HX, 8 * t : 8 * t + 8, :]
            out_ref[x - HX, 8 * t : 8 * t + 8, :] = v + wdiag[x, r : r + 8, :] * (load - q)
        return 0

    lax.fori_loop(HX, HX + TX, finish, 0)


def per_device(facies, source, facies_perm, facies_store, well_x, well_y, well_rate):
    vmem = pl.BlockSpec(memory_space=pltpu.VMEM)
    smem = pl.BlockSpec(memory_space=pltpu.SMEM)
    field = pltpu.VMEM((EX, EY, 128), F32)
    colors = pltpu.VMEM((8, EX, EY, 128), F32)
    return pl.pallas_call(
        kernel,
        out_shape=jax.ShapeDtypeStruct((TX, TY, CELLS_Z), F32),
        in_specs=[vmem, vmem, smem, smem, vmem, vmem, vmem],
        out_specs=vmem,
        scratch_shapes=[
            pltpu.VMEM((EX, EY, 128), jnp.int32),
            field,
            field,
            pltpu.VMEM((12, EX, 24, 128), F32),
            pltpu.VMEM((6, EX, EY, 128), F32),
            field,
            colors,
            colors,
            pltpu.VMEM((8, TX, TY, 128), F32),
            pltpu.VMEM((TX, TY, 128), F32),
            pltpu.VMEM((9, 8, 128), F32),
            pltpu.VMEM((DX, 8, 128), F32),
            pltpu.VMEM((DY, 8, 128), F32),
            pltpu.VMEM((2, 8, 128), F32),
            field,
            pltpu.VMEM((8, 128), F32),
            pltpu.VMEM((8, 128), F32),
            pltpu.SemaphoreType.DMA((8,)),
            pltpu.SemaphoreType.DMA((8,)),
            pltpu.SemaphoreType.DMA((DX,)),
            pltpu.SemaphoreType.DMA((DX,)),
            pltpu.SemaphoreType.DMA((DY,)),
            pltpu.SemaphoreType.DMA((DY,)),
        ],
        compiler_params=pltpu.CompilerParams(
            collective_id=0, has_side_effects=True, vmem_limit_bytes=40 * 1024 * 1024
        ),
    )(
        facies, source, facies_perm, facies_store,
        well_x.reshape(1, WELLS), well_y.reshape(1, WELLS), well_rate.reshape(1, WELLS),
    )


def solution(mesh):
    in_specs = (P("gx", "gy", None), P("gx", "gy", None), P(), P(), P(), P(), P())
    return jax.shard_map(
        per_device, mesh=mesh, in_specs=in_specs, out_specs=P("gx", "gy", None), check_vma=False
    )
```

```python
import functools

import jax
import jax.numpy as jnp
from jax import lax
from jax.experimental import pallas as pl
from jax.experimental.pallas import tpu as pltpu
from jax.sharding import PartitionSpec as P

GRID_X, GRID_Y, CELLS_Z = 128, 256, 128
BLOCK_X, BLOCK_Y, BLOCK_Z = 64, 64, 16
FACIES = 8
WELLS = 64
RELAX = 2.0 / 3.0

TX, TY = 8, 16
HX, HY = 4, 8
EX, EY = TX + 2 * HX, TY + 2 * HY
DX, DY = 16, 16
MESH = pl.DeviceIdType.MESH
F32 = jnp.float32

COLORS = [(c >> 2 & 1, c & 1, c >> 1 & 1) for c in range(8)]


def roll(value, shift):
    return pltpu.roll(value, shift % 128, 1)


def iota(dim):
    return lax.broadcasted_iota(jnp.int32, (8, 128), dim)


def flag(cond):
    return jnp.where(cond, 1.0, 0.0).astype(F32)


def same_xy(coord, parity, block):
    return flag((coord + 1 + block // 2 - block * parity + 4 * block) % (2 * block) != 0)


def same_z(coord, parity):
    return flag((coord + 1 + BLOCK_Z // 2 - BLOCK_Z * parity + 2 * BLOCK_Z) % (2 * BLOCK_Z) != 0)


def inside(coord, total):
    return (coord >= 0) & (coord < total)


def kernel(
    facies_hbm, source_hbm, perm_ref, store_ref, wx_hbm, wy_hbm, wr_hbm, out_ref,
    fac, hperm, stor, coef, trans, wdiag, va, vb, bv, rim, rimy, rhs, wide, stage1, stage2, val, prol,
    mine, half, source_ref, wx_ref, wy_ref, wr_ref,
    insem, hsend, hrecv, xsend, xrecv, ysend, yrecv,
):
    gx = lax.axis_index("gx")
    gy = lax.axis_index("gy")
    ax, ay = gx * TX, gy * TY
    lane, sub = iota(1), iota(0)

    inputs = [
        pltpu.make_async_copy(facies_hbm, fac.at[pl.ds(HX, TX), pl.ds(HY, TY)], insem.at[0]),
        pltpu.make_async_copy(source_hbm, source_ref, insem.at[1]),
        pltpu.make_async_copy(wx_hbm, wx_ref, insem.at[2]),
        pltpu.make_async_copy(wy_hbm, wy_ref, insem.at[3]),
        pltpu.make_async_copy(wr_hbm, wr_ref, insem.at[4]),
    ]
    barrier = pltpu.get_barrier_semaphore()
    near = [((gx + i) % DX, (gy + j) % DY) for i in (0, 1, DX - 1) for j in (0, 1, DY - 1) if i or j]
    far = [((gx + d) % DX, gy) for d in range(2, DX - 1)] + [(gx, (gy + d) % DY) for d in range(2, DY - 1)]
    for who in near + far:
        pl.semaphore_signal(barrier, inc=1, device_id=who, device_id_type=MESH)
    for copy in inputs:
        copy.start()
    pl.semaphore_wait(barrier, len(near) + len(far))

    copies = []
    n = 0
    for dx in (-1, 0, 1):
        for dy in (-1, 0, 1):
            if dx == 0 and dy == 0:
                continue
            sx = {1: (TX - HX, HX), -1: (0, HX), 0: (0, TX)}[dx]
            sy = {1: (TY - HY, HY), -1: (0, HY), 0: (0, TY)}[dy]
            tx = {1: 0, -1: HX + TX, 0: HX}[dx]
            ty = {1: 0, -1: HY + TY, 0: HY}[dy]
            copies.append(
                pltpu.make_async_remote_copy(
                    src_ref=facies_hbm.at[pl.ds(sx[0], sx[1]), pl.ds(sy[0], sy[1])],
                    dst_ref=fac.at[pl.ds(tx, sx[1]), pl.ds(ty, sy[1])],
                    send_sem=hsend.at[n],
                    recv_sem=hrecv.at[n],
                    device_id=((gx + dx + DX) % DX, (gy + dy + DY) % DY),
                    device_id_type=MESH,
                )
            )
            n += 1
    for copy in copies:
        copy.start()

    for copy in inputs[1:]:
        copy.wait()
    well_x = wx_ref[...]
    well_y = wy_ref[...]
    well_r = wr_ref[...]
    sub64 = lax.broadcasted_iota(jnp.int32, (8, WELLS), 0)
    for j in range(2):
        hit_y = jnp.where(sub64 + (ay + 8 * j) == well_y, well_r, 0.0)
        for x in range(TX):
            part = jnp.where(well_x == ax + x, hit_y, 0.0)
            column = jnp.sum(part, axis=1, keepdims=True)
            rhs[x, 8 * j : 8 * j + 8, :] = source_ref[x, 8 * j : 8 * j + 8, :] + column / CELLS_Z

    def start_plane(x, _):
        gxe = ax - HX + x
        for t in range(4):
            row = ay - HY + 8 * t + sub
            for c, (i, j, k) in enumerate(COLORS):
                hit = inside(row, GRID_Y) & ((row // BLOCK_Y) % 2 == j) & ((lane // BLOCK_Z) % 2 == k)
                hitx = inside(gxe, GRID_X) & ((gxe + 2 * BLOCK_X) // BLOCK_X % 2 == i)
                va[c, x, 8 * t : 8 * t + 8, :] = flag(hit) * flag(hitx)
        return 0

    lax.fori_loop(0, EX, start_plane, 0)

    inputs[0].wait()

    half_inv = [0.5 / jnp.full((8, 128), perm_ref[f], F32) for f in range(FACIES)]
    store_at = [jnp.full((8, 128), store_ref[f], F32) for f in range(FACIES)]

    def pick(code, table):
        bits = [(code // (1 << b)) % 2 == 1 for b in range(3)]
        for b in range(3):
            table = [jnp.where(bits[b], hi, lo) for lo, hi in zip(table[::2], table[1::2])]
        return table[0]

    def lookup(tiles):
        def plane(x, _):
            for t in tiles:
                code = fac[x, 8 * t : 8 * t + 8, :]
                hperm[x, 8 * t : 8 * t + 8, :] = pick(code, half_inv)
                stor[x, 8 * t : 8 * t + 8, :] = pick(code, store_at)
            return 0

        return plane

    lax.fori_loop(HX, HX + TX, lookup((1, 2)), 0)
    for copy in copies:
        copy.wait_recv()
    lax.fori_loop(0, HX, lookup(range(4)), 0)
    lax.fori_loop(HX, HX + TX, lookup((0, 3)), 0)
    lax.fori_loop(HX + TX, EX, lookup(range(4)), 0)

    last_z = flag(lane < CELLS_Z - 1)

    def coef_plane(x, _):
        gxe = ax - HX + x
        ok_m = flag(inside(gxe - 1, GRID_X) & inside(gxe, GRID_X))
        ok_p = flag(inside(gxe, GRID_X) & inside(gxe + 1, GRID_X))
        for t in range(3):
            r = 4 + 8 * t
            h = hperm[x, r : r + 8, :]
            row = ay - HY + r + sub
            row_m = flag(inside(row - 1, GRID_Y) & inside(row, GRID_Y))
            row_p = flag(inside(row, GRID_Y) & inside(row + 1, GRID_Y))
            txm = ok_m / (h + hperm[x - 1, r : r + 8, :])
            txp = ok_p / (h + hperm[x + 1, r : r + 8, :])
            tym = row_m / (h + hperm[x, r - 1 : r + 7, :])
            typ = row_p / (h + hperm[x, r + 1 : r + 9, :])
            tzp = last_z / (h + roll(h, -1))
            tzm = roll(tzp, 1)
            diag = stor[x, r : r + 8, :] + txm + txp + tym + typ + tzm + tzp
            w = RELAX / diag
            wdiag[x, r : r + 8, :] = w
            for n, value in enumerate((txm, txp, tym, typ, tzm, tzp)):
                trans[n, x, r : r + 8, :] = value
            wxm, wxp, wym, wyp, wzm, wzp = [w * v for v in (txm, txp, tym, typ, tzm, tzp)]
            a = 8 * t
            for p in range(2):
                coef[p, x, a : a + 8, :] = wxm * same_xy(gxe - 1, p, BLOCK_X)
                coef[2 + p, x, a : a + 8, :] = wxp * same_xy(gxe, p, BLOCK_X)
                coef[4 + p, x, a : a + 8, :] = wym * same_xy(row - 1, p, BLOCK_Y)
                coef[6 + p, x, a : a + 8, :] = wyp * same_xy(row, p, BLOCK_Y)
                coef[8 + p, x, a : a + 8, :] = wzm * same_z(lane - 1, p)
                coef[10 + p, x, a : a + 8, :] = wzp * same_z(lane, p)
        return 0

    lax.fori_loop(1, EX - 1, coef_plane, 0)

    def sweep(src, dst, low):
        def plane(x, _):
            for t in range(3):
                r, a = 4 + 8 * t, 8 * t
                k = [coef[n, x, a : a + 8, :] for n in range(12)]
                old, new = [], []
                for c, (px, py, pz) in enumerate(COLORS):
                    v = src[c, x, r : r + 8, :]
                    q = k[px] * src[c, x - 1, r : r + 8, :] + k[2 + px] * src[c, x + 1, r : r + 8, :]
                    q += k[4 + py] * src[c, x, r - 1 : r + 7, :] + k[6 + py] * src[c, x, r + 1 : r + 9, :]
                    q += k[8 + pz] * roll(v, 1) + k[10 + pz] * roll(v, -1)
                    old.append(v)
                    new.append(q)
                total = functools.reduce(jnp.add, new) - RELAX * functools.reduce(jnp.add, old)
                keep = (1.0 - RELAX) - total
                for c in range(8):
                    dst[c, x, r : r + 8, :] = new[c] + old[c] * keep
            return 0

        lax.fori_loop(low, EX - low, plane, 0)

    sweep(va, vb, 1)
    sweep(vb, va, 2)
    sweep(va, vb, 3)
    basis = vb

    def apply_plane(x, _):
        for t in range(2):
            r = HY + 8 * t
            row = ay + 8 * t + sub
            k = [trans[n, x, r : r + 8, :] for n in range(6)]
            s = stor[x, r : r + 8, :]
            ym = [same_xy(row - 1, p, BLOCK_Y) for p in range(2)]
            yp = [same_xy(row, p, BLOCK_Y) for p in range(2)]
            zm = [same_z(lane - 1, p) for p in range(2)]
            zp = [same_z(lane, p) for p in range(2)]
            for c, (px, py, pz) in enumerate(COLORS):
                v = basis[c, x, r : r + 8, :]
                q = s * v
                q += k[0] * (v - basis[c, x - 1, r : r + 8, :]) + k[1] * (v - basis[c, x + 1, r : r + 8, :])
                q += k[2] * (v - ym[py] * basis[c, x, r - 1 : r + 7, :])
                q += k[3] * (v - yp[py] * basis[c, x, r + 1 : r + 9, :])
                q += k[4] * (v - zm[pz] * roll(v, 1)) + k[5] * (v - zp[pz] * roll(v, -1))
                bv[c, x - HX, 8 * t : 8 * t + 8, :] = q
                rimy[c, x - HX, 8 * t : 8 * t + 8, :] = (
                    (ym[1 - py] - 1.0) * k[2] * basis[c, x, r - 1 : r + 7, :]
                    + (yp[1 - py] - 1.0) * k[3] * basis[c, x, r + 1 : r + 9, :]
                )
        return 0

    lax.fori_loop(HX, HX + TX, apply_plane, 0)

    west = lane < 64
    cut_lo = [1.0 - same_z(lane, p) for p in range(2)]
    cut_hi = [1.0 - same_z(lane - 1, p) for p in range(2)]
    turn = lane % 32 >= 16

    def rim_plane(x, acc):
        acc = list(acc)
        for t in range(2):
            r = HY + 8 * t
            tzm, tzp = trans[4, x, r : r + 8, :], trans[5, x, r : r + 8, :]
            lo = [-tzp * cut_lo[1 - p] for p in range(2)]
            hi = [-tzm * cut_hi[1 - p] for p in range(2)]
            both = -tzp * (cut_lo[0] + cut_lo[1])
            vs = [basis[c, x, r : r + 8, :] for c in range(8)]
            up = [roll(v, -1) for v in vs]
            for c, (px, py, pz) in enumerate(COLORS):
                rim[c, x - HX, 8 * t : 8 * t + 8, :] = lo[pz] * up[c] + hi[pz] * roll(vs[c], 1)
            here = [jnp.where(turn, vs[c], vs[c + 2]) for c in (0, 1, 4, 5)]
            there = [jnp.where(turn, up[c], up[c + 2]) for c in (0, 1, 4, 5)]
            first = [both * jnp.where(west, a, b) for a, b in zip(here, there)]
            second = [jnp.where(west, b, a) for a, b in zip(here, there)]
            for m in range(4):
                for n in range(4):
                    acc[4 * m + n] = acc[4 * m + n] + first[m] * second[n]
        return tuple(acc)

    zeros16 = tuple(jnp.zeros((8, 128), F32) for _ in range(16))
    acc = lax.fori_loop(HX, HX + TX, rim_plane, zeros16)
    for n in range(8, 16):
        wide[n] = jnp.zeros((8, 128), F32)
    corner4 = (0, 1, 4, 5)
    for m in range(4):
        for n in range(4):
            wide[8 + m, corner4[n] : corner4[n] + 1, :] = jnp.sum(acc[4 * m + n], axis=0, keepdims=True)

    parity_y = jnp.where(gy == 9, 1, 0)
    at_rim = jnp.where((gy == 5) | (gy == 9), -1.0, 0.0).astype(F32)
    top = flag(sub == 7) * at_rim

    def rim_y_plane(x, acc):
        acc = list(acc)
        t = trans[3, x, HY + 8 : HY + 16, :] * top
        here = [t * basis[c + parity_y, x, HY + 8 : HY + 16, :] for c in (0, 2, 4, 6)]
        there = [basis[c + parity_y, x, HY + 9 : HY + 17, :] for c in (0, 2, 4, 6)]
        for m in range(4):
            for n in range(4):
                acc[4 * m + n] = acc[4 * m + n] + here[m] * there[n]
        return tuple(acc)

    acc = lax.fori_loop(HX, HX + TX, rim_y_plane, zeros16)
    for m in range(4):
        for n in range(4):
            line = jnp.sum(acc[4 * m + n], axis=0, keepdims=True)
            wide[12 + m, 2 * n : 2 * n + 1, :] = line
            wide[12 + n, 2 * m + 1 : 2 * m + 2, :] = line

    pairs = [(a, c) for a in range(8) for c in range(a, 8)]
    for group in (pairs[:15], pairs[15:30], pairs[30:]):
        rows = sorted({a for a, _ in group})
        cols = sorted({c for _, c in group})
        last = group[-1] == (7, 7)

        def gather(x, acc, group=group, rows=rows, cols=cols, last=last):
            acc = list(acc)
            for t in range(2):
                r = HY + 8 * t
                at = slice(8 * t, 8 * t + 8)
                left = {a: basis[a, x + HX, r : r + 8, :] for a in (range(8) if last else rows)}
                right = {c: bv[c, x, at, :] for c in cols}
                own = {c: basis[c, x + HX, r : r + 8, :] for c in cols}
                over_z = {a: rim[a, x, at, :] for a in rows}
                over_y = {a: rimy[a, x, at, :] for a in rows}
                for n, (a, c) in enumerate(group):
                    acc[n] = acc[n] + left[a] * right[c]
                    if COLORS[a][2] != COLORS[c][2] and COLORS[a][1] != COLORS[c][1]:
                        acc[n] = acc[n] + own[c] * (over_z[a] + over_y[a])
                    elif COLORS[a][2] != COLORS[c][2]:
                        acc[n] = acc[n] + own[c] * over_z[a]
                    elif COLORS[a][1] != COLORS[c][1]:
                        acc[n] = acc[n] + own[c] * over_y[a]
                if last:
                    load = rhs[x, at, :]
                    for a in range(8):
                        acc[len(group) + a] = acc[len(group) + a] + left[a] * load
            return tuple(acc)

        count = len(group) + (8 if last else 0)
        acc = lax.fori_loop(0, TX, gather, tuple(jnp.zeros((8, 128), F32) for _ in range(count)))
        for n, (a, c) in enumerate(group):
            line = jnp.sum(acc[n], axis=0, keepdims=True)
            wide[c, a : a + 1, :] = line
            if a != c:
                wide[a, c : c + 1, :] = line
        if last:
            for a in range(8):
                wide[16, a : a + 1, :] = jnp.sum(acc[len(group) + a], axis=0, keepdims=True)

    def ranges(places):
        total = jnp.zeros((8, 128), F32)
        for n, slot in places:
            line = wide[n]
            for step in (1, 2, 4, 8):
                line = line + roll(line, -step)
            line = jnp.where(lane % 16 == 8, line, 0.0)
            total = total + roll(line, 8 + slot)
        return total

    mine[0:8, :] = ranges([(n, n) for n in range(8)] + [(8 + m, 8 + corner4[m]) for m in range(4)])
    mine[8:16, :] = ranges([(12 + m, 2 * m) for m in range(4)] + [(16, 1)])

    def exchange(src, slots, send, recv, axis):
        me = gx if axis == 0 else gy
        size = DX if axis == 0 else DY
        sent = []
        for d in range(1, size):
            to = ((gx + d) % DX, gy) if axis == 0 else (gx, (gy + d) % DY)
            copy = pltpu.make_async_remote_copy(
                src_ref=src, dst_ref=slots.at[me], send_sem=send.at[d], recv_sem=recv.at[d],
                device_id=to, device_id_type=MESH,
            )
            copy.start()
            sent.append(copy)
        slots[me] = src[...]
        for copy in sent:
            copy.wait_recv()
        return sent

    def tree(items):
        while len(items) > 1:
            items = [a + b for a, b in zip(items[::2], items[1::2])] + (items[-1:] if len(items) % 2 else [])
        return items[0]

    sent = exchange(mine, stage1, xsend, xrecv, 0)
    half[...] = tree([stage1[n] for n in range(DX)])
    sent += exchange(half, stage2, ysend, yrecv, 1)

    def parts(rows):
        return [tree([stage2[n, rows : rows + 8, :] for n in range(*ends)]) for ends in ((0, 6), (6, 10), (10, 16))]

    pa, pb, pc = parts(0)
    qa, qb, qc = parts(8)
    slot = lane % 16
    ly, sy = lane % 2, sub % 2
    lk, sk = lane // 2 % 2, sub // 2 % 2

    def keep(cond, value):
        return jnp.where(cond, value, 0.0)

    def rows_up(value, shift):
        return pltpu.roll(value, shift % 8, 0)

    m00, m01 = (ly == 0) & (sy == 0), (ly == 0) & (sy == 1)
    m10, m11 = (ly == 1) & (sy == 0), (ly == 1) & (sy == 1)
    pairs_y = (slot < 8) & (lk < 2)
    y01 = keep(pairs_y & m00, qa) + keep(pairs_y & m11, rows_up(roll(qb, 1), 1))
    y10 = keep(pairs_y & m00, rows_up(qa, -1)) + keep(pairs_y & m11, roll(qb, 1))
    joined = [[pa + keep(m11, pb), keep(m10, pb) + y01], [keep(m01, pb) + y10, pc + keep(m00, pb)]]
    by_row = []
    for pk in range(2):
        picked = [[keep(lk == pk, joined[h][g]) for g in range(2)] for h in range(2)]
        by_row.append([
            (picked[0][g] + roll(picked[1][g], 2)) if pk == 0 else (roll(picked[0][g], -2) + picked[1][g])
            for g in range(2)
        ])

    def by_column(values, pk):
        low, high = keep(sk == pk, values[0]), keep(sk == pk, values[1])
        return low + rows_up(high, 2) if pk == 0 else rows_up(low, -2) + high

    node = [[by_column(by_row[pk], pq) for pq in range(2)] for pk in range(2)]
    loads = [qa + keep(sy == 1, qb), qc + keep(sy == 0, qb)]
    load_of = [by_column(loads, pk) for pk in range(2)]
    layer = lane // 16
    even = layer % 2 == 0
    own = jnp.where(even, node[0][0] + roll(node[0][0], -16), node[1][1] + roll(node[1][1], -16))
    near_k = jnp.where(even, node[0][1], node[1][0])
    near_up = jnp.where(even, roll(node[0][1], -16), roll(node[1][0], -16))
    near_k = jnp.where(layer < 4, near_up, near_k)
    far_k = jnp.where(layer < 4, roll(node[0][0], -24), roll(node[0][0], 8))
    load_k = jnp.where(even, load_of[0] + roll(load_of[0], -16), load_of[1] + roll(load_of[1], -16))

    def ends(value, level, at):
        a, b = 16 * level + at, 16 * (7 - level) + at
        return jnp.where(west, jnp.broadcast_to(value[:, a : a + 1], (8, 128)), jnp.broadcast_to(value[:, b : b + 1], (8, 128)))

    def all_lanes(value, at):
        return jnp.broadcast_to(value[:, at : at + 1], (8, 128))

    def spread(value, k):
        return jnp.broadcast_to(value[k : k + 1, :], (8, 128))

    def eliminate(block, nexts, load, after):
        block, nexts = list(block), [list(b) for b in nexts]
        load = [spread(load, k) for k in range(8)]
        for k in range(8):
            inverse = 1.0 / spread(block[k], k)
            pivot = block[k] * inverse
            scaled = [b[k] * inverse for b in nexts]
            scaled_load = load[k] * inverse
            after([b[k] for b in nexts], scaled, scaled_load)
            for i in range(8):
                if i == k:
                    continue
                f = spread(block[i], k)
                block[i] = block[i] - f * pivot
                for b, v in zip(nexts, scaled):
                    b[i] = b[i] - f * v
                load[i] = load[i] - f * scaled_load
            block[k] = pivot
            for b, v in zip(nexts, scaled):
                b[k] = v
            load[k] = scaled_load
        return nexts, load

    diag = [[ends(own, l, i) for i in range(8)] for l in range(3)]
    one = [[ends(near_k, l, i) for i in range(8)] for l in range(3)]
    two = [[ends(far_k, l, i) for i in range(8)] for l in range(3)]
    right = [ends(load_k, l, 1) for l in range(3)]
    zero = jnp.zeros((8, 128), F32)
    d3, d4, d34 = [zero] * 8, [zero] * 8, [zero] * 8
    r3, r4 = zero, zero
    solved = []
    for level in range(3):
        def after(raw, scaled, load, level=level):
            nonlocal r3, r4
            p1, p2 = raw
            s1, s2 = scaled
            for i in range(8):
                f1, f2 = spread(p1, i), spread(p2, i)
                if level == 0:
                    diag[1][i] = diag[1][i] - f1 * s1
                    one[1][i] = one[1][i] - f1 * s2
                    diag[2][i] = diag[2][i] - f2 * s2
                elif level == 1:
                    diag[2][i] = diag[2][i] - f1 * s1
                    one[2][i] = one[2][i] - f1 * s2
                    d3[i] = d3[i] - f2 * s2
                else:
                    d3[i] = d3[i] - f1 * s1
                    d4[i] = d4[i] - f2 * s2
                    d34[i] = d34[i] - jnp.where(west, f1, f2) * jnp.where(west, s2, s1)
            if level == 0:
                right[1] = right[1] - p1 * load
                right[2] = right[2] - p2 * load
            elif level == 1:
                right[2] = right[2] - p1 * load
                r3 = r3 - p2 * load
            else:
                r3 = r3 - p1 * load
                r4 = r4 - p2 * load

        solved.append(eliminate(diag[level], [one[level], two[level]], right[level], after))

    def meet(a, b):
        value = jnp.where(west, a, b)
        return value + roll(value, 64)

    m3 = [all_lanes(own, 48 + i) + meet(d3[i], d4[i]) for i in range(8)]
    m4 = [all_lanes(own, 64 + i) + meet(d4[i], d3[i]) for i in range(8)]
    m34 = [all_lanes(near_k, 48 + i) + d34[i] + roll(d34[i], 64) for i in range(8)]
    v3 = all_lanes(load_k, 49) + meet(r3, r4)
    v4 = all_lanes(load_k, 65) + meet(r4, r3)

    def after_three(raw, scaled, load):
        nonlocal v4
        for i in range(8):
            m4[i] = m4[i] - spread(raw[0], i) * scaled[0]
        v4 = v4 - raw[0] * load

    (up3,), load3 = eliminate(m3, [m34], v3, after_three)
    _, x4 = eliminate(m4, [], v4, lambda *_: None)

    def column(items):
        value = items[0]
        for i in range(1, 8):
            value = jnp.where(sub == i, items[i], value)
        return value

    def total(value):
        return jnp.broadcast_to(jnp.sum(value, axis=0, keepdims=True), (8, 128))

    c4 = column(x4)
    x3 = [load3[i] - total(up3[i] * c4) for i in range(8)]
    c3 = column(x3)
    first, second = jnp.where(west, c3, c4), jnp.where(west, c4, c3)
    x_of = [None] * 3
    for level in (2, 1, 0):
        (n1, n2), load = solved[level]
        x_of[level] = [load[i] - total(n1[i] * first + n2[i] * second) for i in range(8)]
        first, second = column(x_of[level]), first

    node_k = [2 * ((lane + BLOCK_Z // 2) // (2 * BLOCK_Z)),
              2 * ((lane + BLOCK_Z // 2 + BLOCK_Z) // (2 * BLOCK_Z)) - 1]
    for p in range(2):
        k = node_k[p]
        at = [((k == level) & west) | ((k == 7 - level) & ~west) for level in range(3)]
        for ij in range(8):
            line = keep(k == 3, x3[ij]) + keep(k == 4, x4[ij])
            for level in range(3):
                line = jnp.where(at[level], x_of[level][ij], line)
            val[p, ij : ij + 1, :] = line[0:1, :]

    def node_row(px, py, pz, tile):
        first = tile * TY
        j = py + 2 * ((first + BLOCK_Y // 2 - BLOCK_Y * py + 4 * BLOCK_Y) // (2 * BLOCK_Y) - 2)
        j = jnp.clip(j, 0, 3)
        return val[pz, pl.ds(4 * px + j, 1), :]

    for t in range(4):
        tile = gy + (-1, 0, 0, 1)[t]
        weights = [jnp.broadcast_to(node_row(px, py, pz, tile), (8, 128)) for px, py, pz in COLORS]

        def prolong(x, _, t=t, weights=weights):
            prol[x, 8 * t : 8 * t + 8, :] = functools.reduce(
                jnp.add, [weights[c] * basis[c, x, 8 * t : 8 * t + 8, :] for c in range(8)]
            )
            return 0

        lax.fori_loop(HX - 1, HX + TX + 1, prolong, 0)

    for copy in copies + sent:
        copy.wait_send()

    def finish(x, _):
        for t in range(2):
            r = HY + 8 * t
            v = prol[x, r : r + 8, :]
            k = [trans[n, x, r : r + 8, :] for n in range(6)]
            q = stor[x, r : r + 8, :] * v
            q += k[0] * (v - prol[x - 1, r : r + 8, :]) + k[1] * (v - prol[x + 1, r : r + 8, :])
            q += k[2] * (v - prol[x, r - 1 : r + 7, :]) + k[3] * (v - prol[x, r + 1 : r + 9, :])
            q += k[4] * (v - roll(v, 1)) + k[5] * (v - roll(v, -1))
            load = rhs[x - HX, 8 * t : 8 * t + 8, :]
            out_ref[x - HX, 8 * t : 8 * t + 8, :] = v + wdiag[x, r : r + 8, :] * (load - q)
        return 0

    lax.fori_loop(HX, HX + TX, finish, 0)


def per_device(facies, source, facies_perm, facies_store, well_x, well_y, well_rate):
    vmem = pl.BlockSpec(memory_space=pltpu.VMEM)
    smem = pl.BlockSpec(memory_space=pltpu.SMEM)
    hbm = pl.BlockSpec(memory_space=pltpu.HBM)
    field = pltpu.VMEM((EX, EY, 128), F32)
    colors = pltpu.VMEM((8, EX, EY, 128), F32)
    return pl.pallas_call(
        kernel,
        out_shape=jax.ShapeDtypeStruct((TX, TY, CELLS_Z), F32),
        in_specs=[hbm, hbm, smem, smem, hbm, hbm, hbm],
        out_specs=vmem,
        scratch_shapes=[
            pltpu.VMEM((EX, EY, 128), jnp.int32),
            field,
            field,
            pltpu.VMEM((12, EX, 24, 128), F32),
            pltpu.VMEM((6, EX, EY, 128), F32),
            field,
            colors,
            colors,
            pltpu.VMEM((8, TX, TY, 128), F32),
            pltpu.VMEM((8, TX, TY, 128), F32),
            pltpu.VMEM((8, TX, TY, 128), F32),
            pltpu.VMEM((TX, TY, 128), F32),
            pltpu.VMEM((17, 8, 128), F32),
            pltpu.VMEM((DX, 16, 128), F32),
            pltpu.VMEM((DY, 16, 128), F32),
            pltpu.VMEM((2, 8, 128), F32),
            field,
            pltpu.VMEM((16, 128), F32),
            pltpu.VMEM((16, 128), F32),
            pltpu.VMEM((TX, TY, 128), F32),
            pltpu.VMEM((1, WELLS), jnp.int32),
            pltpu.VMEM((1, WELLS), jnp.int32),
            pltpu.VMEM((1, WELLS), F32),
            pltpu.SemaphoreType.DMA((5,)),
            pltpu.SemaphoreType.DMA((8,)),
            pltpu.SemaphoreType.DMA((8,)),
            pltpu.SemaphoreType.DMA((DX,)),
            pltpu.SemaphoreType.DMA((DX,)),
            pltpu.SemaphoreType.DMA((DY,)),
            pltpu.SemaphoreType.DMA((DY,)),
        ],
        compiler_params=pltpu.CompilerParams(
            collective_id=0, has_side_effects=True, vmem_limit_bytes=40 * 1024 * 1024
        ),
    )(
        facies, source, facies_perm, facies_store,
        well_x.reshape(1, WELLS), well_y.reshape(1, WELLS), well_rate.reshape(1, WELLS),
    )


def solution(mesh):
    in_specs = (P("gx", "gy", None), P("gx", "gy", None), P(), P(), P(), P(), P())
    return jax.shard_map(
        per_device, mesh=mesh, in_specs=in_specs, out_specs=P("gx", "gy", None), check_vma=False
    )
```

```python
import functools

import jax
import jax.numpy as jnp
from jax import lax
from jax.experimental import pallas as pl
from jax.experimental.pallas import tpu as pltpu
from jax.sharding import PartitionSpec as P

GRID_X, GRID_Y, CELLS_Z = 128, 256, 128
BLOCK_X, BLOCK_Y, BLOCK_Z = 64, 64, 16
FACIES = 8
WELLS = 64
RELAX = 2.0 / 3.0

TX, TY = 8, 16
HX, HY = 4, 8
EX, EY = TX + 2 * HX, TY + 2 * HY
DX, DY = 16, 16
MESH = pl.DeviceIdType.MESH
UNROLL_SWEEP, UNROLL_COEF = True, 2
F32 = jnp.float32

COLORS = [(c >> 2 & 1, c & 1, c >> 1 & 1) for c in range(8)]


def roll(value, shift):
    return pltpu.roll(value, shift % 128, 1)


def iota(dim):
    return lax.broadcasted_iota(jnp.int32, (8, 128), dim)


def flag(cond):
    return jnp.where(cond, 1.0, 0.0).astype(F32)


def same_xy(coord, parity, block):
    return flag((coord + 1 + block // 2 - block * parity + 4 * block) % (2 * block) != 0)


def same_z(coord, parity):
    return flag((coord + 1 + BLOCK_Z // 2 - BLOCK_Z * parity + 2 * BLOCK_Z) % (2 * BLOCK_Z) != 0)


def inside(coord, total):
    return (coord >= 0) & (coord < total)


def kernel(
    facies_hbm, source_hbm, perm_ref, store_ref, wx_hbm, wy_hbm, wr_hbm, out_ref,
    fac, hperm, stor, coef, trans, wdiag, va, vb, bv, rim, rimy, rhs, wide, stage1, stage2, val, prol,
    mine, half, source_ref, wx_ref, wy_ref, wr_ref,
    insem, hsend, hrecv, xsend, xrecv, ysend, yrecv, news_x, news_y,
):
    gx = lax.axis_index("gx")
    gy = lax.axis_index("gy")
    ax, ay = gx * TX, gy * TY
    lane, sub = iota(1), iota(0)

    inputs = [
        pltpu.make_async_copy(facies_hbm, fac.at[pl.ds(HX, TX), pl.ds(HY, TY)], insem.at[0]),
        pltpu.make_async_copy(source_hbm, source_ref, insem.at[1]),
        pltpu.make_async_copy(wx_hbm, wx_ref, insem.at[2]),
        pltpu.make_async_copy(wy_hbm, wy_ref, insem.at[3]),
        pltpu.make_async_copy(wr_hbm, wr_ref, insem.at[4]),
    ]
    barrier = pltpu.get_barrier_semaphore()
    near = [((gx + i) % DX, (gy + j) % DY) for i in (0, 1, DX - 1) for j in (0, 1, DY - 1) if i or j]
    for who in near:
        pl.semaphore_signal(barrier, inc=1, device_id=who, device_id_type=MESH)
    for copy in inputs:
        copy.start()
    pl.semaphore_wait(barrier, len(near))

    def tell(n):
        d = 1 << n
        for i in (d, DX - d):
            pl.semaphore_signal(news_x.at[n], inc=1, device_id=((gx + i) % DX, gy), device_id_type=MESH)
        for j in (d, DY - d):
            pl.semaphore_signal(news_y.at[n], inc=1, device_id=(gx, (gy + j) % DY), device_id_type=MESH)

    def hear(n):
        pl.semaphore_wait(news_x.at[n], 2)
        pl.semaphore_wait(news_y.at[n], 2)

    copies = []
    n = 0
    for dx in (-1, 0, 1):
        for dy in (-1, 0, 1):
            if dx == 0 and dy == 0:
                continue
            wx = HX if dy == 0 else HX - 1
            sx = {1: (TX - wx, wx), -1: (0, wx), 0: (0, TX)}[dx]
            sy = {1: (TY - 4, 4), -1: (0, 4), 0: (0, TY)}[dy]
            tx = {1: HX - wx, -1: HX + TX, 0: HX}[dx]
            ty = {1: HY - 4, -1: HY + TY, 0: HY}[dy]
            copies.append(
                pltpu.make_async_remote_copy(
                    src_ref=facies_hbm.at[pl.ds(sx[0], sx[1]), pl.ds(sy[0], sy[1])],
                    dst_ref=fac.at[pl.ds(tx, sx[1]), pl.ds(ty, sy[1])],
                    send_sem=hsend.at[n],
                    recv_sem=hrecv.at[n],
                    device_id=((gx + dx + DX) % DX, (gy + dy + DY) % DY),
                    device_id_type=MESH,
                )
            )
            n += 1
    for copy in copies:
        copy.start()
    tell(0)

    for copy in inputs[1:]:
        copy.wait()
    well_x = wx_ref[...]
    well_y = wy_ref[...]
    well_r = wr_ref[...]
    sub64 = lax.broadcasted_iota(jnp.int32, (8, WELLS), 0)
    for j in range(2):
        hit_y = jnp.where(sub64 + (ay + 8 * j) == well_y, well_r, 0.0)
        for x in range(TX):
            part = jnp.where(well_x == ax + x, hit_y, 0.0)
            column = jnp.sum(part, axis=1, keepdims=True)
            rhs[x, 8 * j : 8 * j + 8, :] = source_ref[x, 8 * j : 8 * j + 8, :] + column / CELLS_Z

    last_z = flag(lane < CELLS_Z - 1)
    row_at = [ay - HY + 4 + 8 * t + sub for t in range(3)]
    row_m = [flag(inside(row - 1, GRID_Y) & inside(row, GRID_Y)) for row in row_at]
    row_p = [flag(inside(row, GRID_Y) & inside(row + 1, GRID_Y)) for row in row_at]
    same_ym = [[same_xy(row - 1, p, BLOCK_Y) for p in range(2)] for row in row_at]
    same_yp = [[same_xy(row, p, BLOCK_Y) for p in range(2)] for row in row_at]
    same_zm = [same_z(lane - 1, p) for p in range(2)]
    same_zp = [same_z(lane, p) for p in range(2)]

    def start_plane(x, _):
        gxe = ax - HX + x
        for t in range(4):
            row = ay - HY + 8 * t + sub
            for c, (i, j, k) in enumerate(COLORS):
                hit = inside(row, GRID_Y) & ((row // BLOCK_Y) % 2 == j) & ((lane // BLOCK_Z) % 2 == k)
                hitx = inside(gxe, GRID_X) & ((gxe + 2 * BLOCK_X) // BLOCK_X % 2 == i)
                va[c, x, 8 * t : 8 * t + 8, :] = flag(hit) * flag(hitx)
        return 0

    lax.fori_loop(0, EX, start_plane, 0)

    inputs[0].wait()

    half_inv = [0.5 / jnp.full((8, 128), perm_ref[f], F32) for f in range(FACIES)]
    store_at = [jnp.full((8, 128), store_ref[f], F32) for f in range(FACIES)]

    def pick(code, table):
        bits = [(code // (1 << b)) % 2 == 1 for b in range(3)]
        for b in range(3):
            table = [jnp.where(bits[b], hi, lo) for lo, hi in zip(table[::2], table[1::2])]
        return table[0]

    def lookup(tiles):
        def plane(x, _):
            for t in tiles:
                code = fac[x, 8 * t : 8 * t + 8, :]
                hperm[x, 8 * t : 8 * t + 8, :] = pick(code, half_inv)
                stor[x, 8 * t : 8 * t + 8, :] = pick(code, store_at)
            return 0

        return plane

    lax.fori_loop(HX, HX + TX, lookup((1, 2)), 0)
    for copy in copies:
        copy.wait_recv()
    lax.fori_loop(0, HX, lookup(range(4)), 0)
    lax.fori_loop(HX, HX + TX, lookup((0, 3)), 0)
    lax.fori_loop(HX + TX, EX, lookup(range(4)), 0)

    hear(0)
    tell(1)

    def coef_plane(x, _):
        gxe = ax - HX + x
        ok_m = flag(inside(gxe - 1, GRID_X) & inside(gxe, GRID_X))
        ok_p = flag(inside(gxe, GRID_X) & inside(gxe + 1, GRID_X))
        for t in range(3):
            r = 4 + 8 * t
            h = hperm[x, r : r + 8, :]
            txm = ok_m / (h + hperm[x - 1, r : r + 8, :])
            txp = ok_p / (h + hperm[x + 1, r : r + 8, :])
            tym = row_m[t] / (h + hperm[x, r - 1 : r + 7, :])
            typ = row_p[t] / (h + hperm[x, r + 1 : r + 9, :])
            tzp = last_z / (h + roll(h, -1))
            tzm = roll(tzp, 1)
            diag = stor[x, r : r + 8, :] + txm + txp + tym + typ + tzm + tzp
            w = RELAX / diag
            wdiag[x, r : r + 8, :] = w
            for n, value in enumerate((txm, txp, tym, typ, tzm, tzp)):
                trans[n, x, r : r + 8, :] = value
            wxm, wxp, wym, wyp, wzm, wzp = [w * v for v in (txm, txp, tym, typ, tzm, tzp)]
            a = 8 * t
            for p in range(2):
                coef[p, x, a : a + 8, :] = wxm * same_xy(gxe - 1, p, BLOCK_X)
                coef[2 + p, x, a : a + 8, :] = wxp * same_xy(gxe, p, BLOCK_X)
                coef[4 + p, x, a : a + 8, :] = wym * same_ym[t][p]
                coef[6 + p, x, a : a + 8, :] = wyp * same_yp[t][p]
                coef[8 + p, x, a : a + 8, :] = wzm * same_zm[p]
                coef[10 + p, x, a : a + 8, :] = wzp * same_zp[p]
        return 0

    lax.fori_loop(1, EX - 1, coef_plane, 0, unroll=UNROLL_COEF)

    def sweep(src, dst, low):
        def plane(x, _):
            for t in range(3):
                r, a = 4 + 8 * t, 8 * t
                k = [coef[n, x, a : a + 8, :] for n in range(12)]
                old, new = [], []
                for c, (px, py, pz) in enumerate(COLORS):
                    v = src[c, x, r : r + 8, :]
                    q = k[px] * src[c, x - 1, r : r + 8, :] + k[2 + px] * src[c, x + 1, r : r + 8, :]
                    q += k[4 + py] * src[c, x, r - 1 : r + 7, :] + k[6 + py] * src[c, x, r + 1 : r + 9, :]
                    q += k[8 + pz] * roll(v, 1) + k[10 + pz] * roll(v, -1)
                    old.append(v)
                    new.append(q)
                total = functools.reduce(jnp.add, new) - RELAX * functools.reduce(jnp.add, old)
                keep = (1.0 - RELAX) - total
                for c in range(8):
                    dst[c, x, r : r + 8, :] = new[c] + old[c] * keep
            return 0

        lax.fori_loop(low, EX - low, plane, 0, unroll=UNROLL_SWEEP)

    sweep(va, vb, 1)
    hear(1)
    tell(2)
    sweep(vb, va, 2)
    sweep(va, vb, 3)
    basis = vb

    tile_rows = [ay + 8 * t + sub for t in range(2)]
    tile_ym = [[same_xy(row - 1, p, BLOCK_Y) for p in range(2)] for row in tile_rows]
    tile_yp = [[same_xy(row, p, BLOCK_Y) for p in range(2)] for row in tile_rows]

    def apply_plane(x, _):
        for t in range(2):
            r = HY + 8 * t
            k = [trans[n, x, r : r + 8, :] for n in range(6)]
            s = stor[x, r : r + 8, :]
            ym, yp, zm, zp = tile_ym[t], tile_yp[t], same_zm, same_zp
            for c, (px, py, pz) in enumerate(COLORS):
                v = basis[c, x, r : r + 8, :]
                q = s * v
                q += k[0] * (v - basis[c, x - 1, r : r + 8, :]) + k[1] * (v - basis[c, x + 1, r : r + 8, :])
                q += k[2] * (v - ym[py] * basis[c, x, r - 1 : r + 7, :])
                q += k[3] * (v - yp[py] * basis[c, x, r + 1 : r + 9, :])
                q += k[4] * (v - zm[pz] * roll(v, 1)) + k[5] * (v - zp[pz] * roll(v, -1))
                bv[c, x - HX, 8 * t : 8 * t + 8, :] = q
                rimy[c, x - HX, 8 * t : 8 * t + 8, :] = (
                    (ym[1 - py] - 1.0) * k[2] * basis[c, x, r - 1 : r + 7, :]
                    + (yp[1 - py] - 1.0) * k[3] * basis[c, x, r + 1 : r + 9, :]
                )
        return 0

    lax.fori_loop(HX, HX + TX, apply_plane, 0, unroll=2)

    west = lane < 64
    cut_lo = [1.0 - same_z(lane, p) for p in range(2)]
    cut_hi = [1.0 - same_z(lane - 1, p) for p in range(2)]
    turn = lane % 32 >= 16

    def rim_plane(x, acc):
        acc = list(acc)
        for t in range(2):
            r = HY + 8 * t
            tzm, tzp = trans[4, x, r : r + 8, :], trans[5, x, r : r + 8, :]
            lo = [-tzp * cut_lo[1 - p] for p in range(2)]
            hi = [-tzm * cut_hi[1 - p] for p in range(2)]
            both = -tzp * (cut_lo[0] + cut_lo[1])
            vs = [basis[c, x, r : r + 8, :] for c in range(8)]
            up = [roll(v, -1) for v in vs]
            for c, (px, py, pz) in enumerate(COLORS):
                rim[c, x - HX, 8 * t : 8 * t + 8, :] = lo[pz] * up[c] + hi[pz] * roll(vs[c], 1)
            here = [jnp.where(turn, vs[c], vs[c + 2]) for c in (0, 1, 4, 5)]
            there = [jnp.where(turn, up[c], up[c + 2]) for c in (0, 1, 4, 5)]
            first = [both * jnp.where(west, a, b) for a, b in zip(here, there)]
            second = [jnp.where(west, b, a) for a, b in zip(here, there)]
            for m in range(4):
                for n in range(4):
                    acc[4 * m + n] = acc[4 * m + n] + first[m] * second[n]
        return tuple(acc)

    zeros16 = tuple(jnp.zeros((8, 128), F32) for _ in range(16))
    acc = lax.fori_loop(HX, HX + TX, rim_plane, zeros16, unroll=2)
    for n in range(8, 12):
        wide[n] = jnp.zeros((8, 128), F32)
    corner4, edge4 = (0, 1, 4, 5), (2, 3, 6, 7)
    for m in range(4):
        for n in range(4):
            wide[8 + m, corner4[n] : corner4[n] + 1, :] = jnp.sum(acc[4 * m + n], axis=0, keepdims=True)

    parity_y = jnp.where(gy == 9, 1, 0)
    at_rim = jnp.where((gy == 5) | (gy == 9), -1.0, 0.0).astype(F32)
    top = flag(sub == 7) * at_rim

    def rim_y_plane(x, acc):
        acc = list(acc)
        t = trans[3, x, HY + 8 : HY + 16, :] * top
        here = [t * basis[c + parity_y, x, HY + 8 : HY + 16, :] for c in (0, 2, 4, 6)]
        there = [basis[c + parity_y, x, HY + 9 : HY + 17, :] for c in (0, 2, 4, 6)]
        for m in range(4):
            for n in range(4):
                acc[4 * m + n] = acc[4 * m + n] + here[m] * there[n]
        return tuple(acc)

    acc = lax.fori_loop(HX, HX + TX, rim_y_plane, zeros16, unroll=2)
    for m in range(4):
        for n in range(4):
            line = jnp.sum(acc[4 * m + n], axis=0, keepdims=True)
            wide[12 + m, 2 * n : 2 * n + 1, :] = line
            wide[12 + n, 2 * m + 1 : 2 * m + 2, :] = line

    pairs = [(a, c) for a in range(8) for c in range(a, 8)]
    for group in (pairs[:15], pairs[15:30], pairs[30:]):
        rows = sorted({a for a, _ in group})
        cols = sorted({c for _, c in group})
        last = group[-1] == (7, 7)

        def gather(x, acc, group=group, rows=rows, cols=cols, last=last):
            acc = list(acc)
            for t in range(2):
                r = HY + 8 * t
                at = slice(8 * t, 8 * t + 8)
                left = {a: basis[a, x + HX, r : r + 8, :] for a in (range(8) if last else rows)}
                right = {c: bv[c, x, at, :] for c in cols}
                own = {c: basis[c, x + HX, r : r + 8, :] for c in cols}
                over_z = {a: rim[a, x, at, :] for a in rows}
                over_y = {a: rimy[a, x, at, :] for a in rows}
                for n, (a, c) in enumerate(group):
                    acc[n] = acc[n] + left[a] * right[c]
                    if COLORS[a][2] != COLORS[c][2] and COLORS[a][1] != COLORS[c][1]:
                        acc[n] = acc[n] + own[c] * (over_z[a] + over_y[a])
                    elif COLORS[a][2] != COLORS[c][2]:
                        acc[n] = acc[n] + own[c] * over_z[a]
                    elif COLORS[a][1] != COLORS[c][1]:
                        acc[n] = acc[n] + own[c] * over_y[a]
                if last:
                    load = rhs[x, at, :]
                    for a in range(8):
                        acc[len(group) + a] = acc[len(group) + a] + left[a] * load
            return tuple(acc)

        count = len(group) + (8 if last else 0)
        acc = lax.fori_loop(0, TX, gather, tuple(jnp.zeros((8, 128), F32) for _ in range(count)), unroll=2)
        for n, (a, c) in enumerate(group):
            line = jnp.sum(acc[n], axis=0, keepdims=True)
            wide[c, a : a + 1, :] = line
            if a != c:
                wide[a, c : c + 1, :] = line
        if last:
            for a in range(8):
                at = (8, a) if a in edge4 else (9, a + 2)
                wide[at[0], at[1] : at[1] + 1, :] = jnp.sum(acc[len(group) + a], axis=0, keepdims=True)

    def ranges(places):
        total = jnp.zeros((8, 128), F32)
        for n, slot in places:
            line = wide[n]
            for step in (1, 2, 4, 8):
                line = line + roll(line, -step)
            line = jnp.where(lane % 16 == 8, line, 0.0)
            total = total + roll(line, 8 + slot)
        return total

    mine[...] = ranges(
        [(n, n) for n in range(8)] + [(8 + m, 8 + corner4[m]) for m in range(4)] + [(12 + m, 8 + edge4[m]) for m in range(4)]
    )
    hear(2)

    def exchange(src, slots, send, recv, axis):
        me = gx if axis == 0 else gy
        size = DX if axis == 0 else DY
        for d in range(1, size):
            to = ((gx + d) % DX, gy) if axis == 0 else (gx, (gy + d) % DY)
            pltpu.make_async_remote_copy(
                src_ref=src, dst_ref=slots.at[me], send_sem=send, recv_sem=recv,
                device_id=to, device_id_type=MESH,
            ).start()
        slots[me] = src[...]
        arrived = slots.at[pl.ds(0, size - 1)]
        pltpu.make_async_copy(arrived, arrived, recv).wait()
        return pltpu.make_async_copy(arrived, arrived, send)

    def tree(items):
        while len(items) > 1:
            items = [a + b for a, b in zip(items[::2], items[1::2])] + (items[-1:] if len(items) % 2 else [])
        return items[0]

    sent_x = exchange(mine, stage1, xsend, xrecv, 0)
    half[...] = tree([stage1[n] for n in range(DX)])
    sent_y = exchange(half, stage2, ysend, yrecv, 1)

    pa, pb, pc = [tree([stage2[n] for n in range(*ends)]) for ends in ((0, 6), (6, 10), (10, 16))]
    slot = lane % 16
    ly, sy = lane % 2, sub % 2
    lk, sk = lane // 2 % 2, sub // 2 % 2

    def keep(cond, value):
        return jnp.where(cond, value, 0.0)

    def rows_up(value, shift):
        return pltpu.roll(value, shift % 8, 0)

    m00, m01 = (ly == 0) & (sy == 0), (ly == 0) & (sy == 1)
    m10, m11 = (ly == 1) & (sy == 0), (ly == 1) & (sy == 1)
    qa, qb = [keep(slot % 4 == 0, roll(p, -10)) + keep(slot % 4 == 2, roll(p, -9)) for p in (pa, pb)]
    pairs_y = slot < 8
    y01 = keep(pairs_y & m00, qa) + keep(pairs_y & m11, rows_up(roll(qb, 1), 1))
    y10 = keep(pairs_y & m00, rows_up(qa, -1)) + keep(pairs_y & m11, roll(qb, 1))
    joined = [[pa + keep(m11, pb), keep(m10, pb) + y01], [keep(m01, pb) + y10, pc + keep(m00, pb)]]
    by_row = []
    for pk in range(2):
        picked = [[keep(lk == pk, joined[h][g]) for g in range(2)] for h in range(2)]
        by_row.append([
            (picked[0][g] + roll(picked[1][g], 2)) if pk == 0 else (roll(picked[0][g], -2) + picked[1][g])
            for g in range(2)
        ])

    def by_column(values, pk):
        low, high = keep(sk == pk, values[0]), keep(sk == pk, values[1])
        return low + rows_up(high, 2) if pk == 0 else rows_up(low, -2) + high

    node = [[by_column(by_row[pk], pq) for pq in range(2)] for pk in range(2)]
    loads = [pa + keep(sy == 1, pb), pc + keep(sy == 0, pb)]
    load_of = [
        keep(sk == 0, rows_up(roll(loads[0], -8), -2)) + keep(sk == 1, roll(loads[1], -8)),
        rows_up(keep(sk == 1, roll(loads[0], -7)), -2) + keep(sk == 1, roll(loads[1], -7)),
    ]
    layer = lane // 16
    even = layer % 2 == 0
    own = jnp.where(even, node[0][0] + roll(node[0][0], -16), node[1][1] + roll(node[1][1], -16))
    near_k = jnp.where(even, node[0][1], node[1][0])
    near_up = jnp.where(even, roll(node[0][1], -16), roll(node[1][0], -16))
    near_k = jnp.where(layer < 4, near_up, near_k)
    far_k = jnp.where(layer < 4, roll(node[0][0], -24), roll(node[0][0], 8))
    load_k = jnp.where(even, load_of[0] + roll(load_of[0], -16), load_of[1] + roll(load_of[1], -16))

    def ends(value, level, at):
        a, b = 16 * level + at, 16 * (7 - level) + at
        return jnp.where(west, jnp.broadcast_to(value[:, a : a + 1], (8, 128)), jnp.broadcast_to(value[:, b : b + 1], (8, 128)))

    def all_lanes(value, at):
        return jnp.broadcast_to(value[:, at : at + 1], (8, 128))

    def spread(value, k):
        return jnp.broadcast_to(value[k : k + 1, :], (8, 128))

    def eliminate(block, nexts, load, after):
        block, nexts = list(block), [list(b) for b in nexts]
        load = [spread(load, k) for k in range(8)]
        for k in range(8):
            inverse = 1.0 / spread(block[k], k)
            pivot = block[k] * inverse
            scaled = [b[k] * inverse for b in nexts]
            scaled_load = load[k] * inverse
            after([b[k] for b in nexts], scaled, scaled_load)
            for i in range(8):
                if i == k:
                    continue
                f = spread(block[i], k)
                block[i] = block[i] - f * pivot
                for b, v in zip(nexts, scaled):
                    b[i] = b[i] - f * v
                load[i] = load[i] - f * scaled_load
            block[k] = pivot
            for b, v in zip(nexts, scaled):
                b[k] = v
            load[k] = scaled_load
        return nexts, load

    diag = [[ends(own, l, i) for i in range(8)] for l in range(3)]
    one = [[ends(near_k, l, i) for i in range(8)] for l in range(3)]
    two = [[ends(far_k, l, i) for i in range(8)] for l in range(3)]
    right = [ends(load_k, l, 1) for l in range(3)]
    zero = jnp.zeros((8, 128), F32)
    d3, d4, d34 = [zero] * 8, [zero] * 8, [zero] * 8
    r3, r4 = zero, zero
    solved = []
    for level in range(3):
        def after(raw, scaled, load, level=level):
            nonlocal r3, r4
            p1, p2 = raw
            s1, s2 = scaled
            for i in range(8):
                f1, f2 = spread(p1, i), spread(p2, i)
                if level == 0:
                    diag[1][i] = diag[1][i] - f1 * s1
                    one[1][i] = one[1][i] - f1 * s2
                    diag[2][i] = diag[2][i] - f2 * s2
                elif level == 1:
                    diag[2][i] = diag[2][i] - f1 * s1
                    one[2][i] = one[2][i] - f1 * s2
                    d3[i] = d3[i] - f2 * s2
                else:
                    d3[i] = d3[i] - f1 * s1
                    d4[i] = d4[i] - f2 * s2
                    d34[i] = d34[i] - jnp.where(west, f1, f2) * jnp.where(west, s2, s1)
            if level == 0:
                right[1] = right[1] - p1 * load
                right[2] = right[2] - p2 * load
            elif level == 1:
                right[2] = right[2] - p1 * load
                r3 = r3 - p2 * load
            else:
                r3 = r3 - p1 * load
                r4 = r4 - p2 * load

        solved.append(eliminate(diag[level], [one[level], two[level]], right[level], after))

    def meet(a, b):
        value = jnp.where(west, a, b)
        return value + roll(value, 64)

    m3 = [all_lanes(own, 48 + i) + meet(d3[i], d4[i]) for i in range(8)]
    m4 = [all_lanes(own, 64 + i) + meet(d4[i], d3[i]) for i in range(8)]
    m34 = [all_lanes(near_k, 48 + i) + d34[i] + roll(d34[i], 64) for i in range(8)]
    v3 = all_lanes(load_k, 49) + meet(r3, r4)
    v4 = all_lanes(load_k, 65) + meet(r4, r3)

    def after_three(raw, scaled, load):
        nonlocal v4
        for i in range(8):
            m4[i] = m4[i] - spread(raw[0], i) * scaled[0]
        v4 = v4 - raw[0] * load

    (up3,), load3 = eliminate(m3, [m34], v3, after_three)
    _, x4 = eliminate(m4, [], v4, lambda *_: None)

    def column(items):
        value = items[0]
        for i in range(1, 8):
            value = jnp.where(sub == i, items[i], value)
        return value

    def total(value):
        return jnp.broadcast_to(jnp.sum(value, axis=0, keepdims=True), (8, 128))

    c4 = column(x4)
    x3 = [load3[i] - total(up3[i] * c4) for i in range(8)]
    c3 = column(x3)
    first, second = jnp.where(west, c3, c4), jnp.where(west, c4, c3)
    x_of = [None] * 3
    for level in (2, 1, 0):
        (n1, n2), load = solved[level]
        x_of[level] = [load[i] - total(n1[i] * first + n2[i] * second) for i in range(8)]
        first, second = column(x_of[level]), first

    node_k = [2 * ((lane + BLOCK_Z // 2) // (2 * BLOCK_Z)),
              2 * ((lane + BLOCK_Z // 2 + BLOCK_Z) // (2 * BLOCK_Z)) - 1]
    for p in range(2):
        k = node_k[p]
        at = [((k == level) & west) | ((k == 7 - level) & ~west) for level in range(3)]
        for ij in range(8):
            line = keep(k == 3, x3[ij]) + keep(k == 4, x4[ij])
            for level in range(3):
                line = jnp.where(at[level], x_of[level][ij], line)
            val[p, ij : ij + 1, :] = line[0:1, :]

    def node_row(px, py, pz, tile):
        first = tile * TY
        j = py + 2 * ((first + BLOCK_Y // 2 - BLOCK_Y * py + 4 * BLOCK_Y) // (2 * BLOCK_Y) - 2)
        j = jnp.clip(j, 0, 3)
        return val[pz, pl.ds(4 * px + j, 1), :]

    before, here, beyond = [[node_row(px, py, pz, gy + d) for px, py, pz in COLORS] for d in (-1, 0, 1)]
    for t in range(3):
        r = HY - 1 + 8 * t
        first, others = ((before, here), (here, here), (here, beyond))[t]
        weights = [jnp.where(sub == 0, a, b) for a, b in zip(first, others)]

        def prolong(x, _, r=r, weights=weights):
            prol[x, r : r + 8, :] = functools.reduce(
                jnp.add, [weights[c] * basis[c, x, r : r + 8, :] for c in range(8)]
            )
            return 0

        lax.fori_loop(HX - 1, HX + TX + 1, prolong, 0, unroll=5)

    for copy in copies:
        copy.wait_send()
    sent_x.wait()
    sent_y.wait()

    def finish(x, _):
        for t in range(2):
            r = HY + 8 * t
            v = prol[x, r : r + 8, :]
            k = [trans[n, x, r : r + 8, :] for n in range(6)]
            q = stor[x, r : r + 8, :] * v
            q += k[0] * (v - prol[x - 1, r : r + 8, :]) + k[1] * (v - prol[x + 1, r : r + 8, :])
            q += k[2] * (v - prol[x, r - 1 : r + 7, :]) + k[3] * (v - prol[x, r + 1 : r + 9, :])
            q += k[4] * (v - roll(v, 1)) + k[5] * (v - roll(v, -1))
            load = rhs[x - HX, 8 * t : 8 * t + 8, :]
            out_ref[x - HX, 8 * t : 8 * t + 8, :] = v + wdiag[x, r : r + 8, :] * (load - q)
        return 0

    lax.fori_loop(HX, HX + TX, finish, 0, unroll=2)


def per_device(facies, source, facies_perm, facies_store, well_x, well_y, well_rate):
    vmem = pl.BlockSpec(memory_space=pltpu.VMEM)
    smem = pl.BlockSpec(memory_space=pltpu.SMEM)
    hbm = pl.BlockSpec(memory_space=pltpu.HBM)
    field = pltpu.VMEM((EX, EY, 128), F32)
    colors = pltpu.VMEM((8, EX, EY, 128), F32)
    return pl.pallas_call(
        kernel,
        out_shape=jax.ShapeDtypeStruct((TX, TY, CELLS_Z), F32),
        in_specs=[hbm, hbm, smem, smem, hbm, hbm, hbm],
        out_specs=vmem,
        scratch_shapes=[
            pltpu.VMEM((EX, EY, 128), jnp.int32),
            field,
            field,
            pltpu.VMEM((12, EX, 24, 128), F32),
            pltpu.VMEM((6, EX, EY, 128), F32),
            field,
            colors,
            colors,
            pltpu.VMEM((8, TX, TY, 128), F32),
            pltpu.VMEM((8, TX, TY, 128), F32),
            pltpu.VMEM((8, TX, TY, 128), F32),
            pltpu.VMEM((TX, TY, 128), F32),
            pltpu.VMEM((16, 8, 128), F32),
            pltpu.VMEM((DX, 8, 128), F32),
            pltpu.VMEM((DY, 8, 128), F32),
            pltpu.VMEM((2, 8, 128), F32),
            field,
            pltpu.VMEM((8, 128), F32),
            pltpu.VMEM((8, 128), F32),
            pltpu.VMEM((TX, TY, 128), F32),
            pltpu.VMEM((1, WELLS), jnp.int32),
            pltpu.VMEM((1, WELLS), jnp.int32),
            pltpu.VMEM((1, WELLS), F32),
            pltpu.SemaphoreType.DMA((5,)),
            pltpu.SemaphoreType.DMA((8,)),
            pltpu.SemaphoreType.DMA((8,)),
            pltpu.SemaphoreType.DMA,
            pltpu.SemaphoreType.DMA,
            pltpu.SemaphoreType.DMA,
            pltpu.SemaphoreType.DMA,
            pltpu.SemaphoreType.REGULAR((3,)),
            pltpu.SemaphoreType.REGULAR((3,)),
        ],
        compiler_params=pltpu.CompilerParams(
            collective_id=0, has_side_effects=True, vmem_limit_bytes=40 * 1024 * 1024
        ),
    )(
        facies, source, facies_perm, facies_store,
        well_x.reshape(1, WELLS), well_y.reshape(1, WELLS), well_rate.reshape(1, WELLS),
    )


def solution(mesh):
    in_specs = (P("gx", "gy", None), P("gx", "gy", None), P(), P(), P(), P(), P())
    return jax.shard_map(
        per_device, mesh=mesh, in_specs=in_specs, out_specs=P("gx", "gy", None), check_vma=False
    )
```

```python
import functools

import jax
import jax.numpy as jnp
from jax import lax
from jax.experimental import pallas as pl
from jax.experimental.pallas import tpu as pltpu
from jax.sharding import PartitionSpec as P

GRID_X, GRID_Y, CELLS_Z = 128, 256, 128
BLOCK_X, BLOCK_Y, BLOCK_Z = 64, 64, 16
FACIES = 8
WELLS = 64
RELAX = 2.0 / 3.0

TX, TY = 8, 16
HX, HY = 4, 8
EX, EY = TX + 2 * HX, TY + 2 * HY
DX, DY = 16, 16
MESH = pl.DeviceIdType.MESH
UNROLL_SWEEP, UNROLL_COEF = True, 2
F32 = jnp.float32

COLORS = [(c >> 2 & 1, c & 1, c >> 1 & 1) for c in range(8)]


def roll(value, shift):
    return pltpu.roll(value, shift % 128, 1)


def iota(dim):
    return lax.broadcasted_iota(jnp.int32, (8, 128), dim)


def flag(cond):
    return jnp.where(cond, 1.0, 0.0).astype(F32)


def same_xy(coord, parity, block):
    return flag((coord + 1 + block // 2 - block * parity + 4 * block) % (2 * block) != 0)


def same_z(coord, parity):
    return flag((coord + 1 + BLOCK_Z // 2 - BLOCK_Z * parity + 2 * BLOCK_Z) % (2 * BLOCK_Z) != 0)


def inside(coord, total):
    return (coord >= 0) & (coord < total)


def kernel(
    facies_hbm, source_hbm, perm_ref, store_ref, wx_hbm, wy_hbm, wr_hbm, out_ref,
    fac, hperm, stor, coef, trans, wdiag, va, vb, bv, rim, rimy, rhs, wide, stage1, stage2, val, prol,
    mine, half, source_ref, wx_ref, wy_ref, wr_ref,
    insem, hsend, hrecv, xsend, xrecv, ysend, yrecv, news,
):
    gx = lax.axis_index("gx")
    gy = lax.axis_index("gy")
    ax, ay = gx * TX, gy * TY
    lane, sub = iota(1), iota(0)

    inputs = [
        pltpu.make_async_copy(facies_hbm, fac.at[pl.ds(HX, TX), pl.ds(HY, TY)], insem.at[0]),
        pltpu.make_async_copy(source_hbm, source_ref, insem.at[1]),
        pltpu.make_async_copy(wx_hbm, wx_ref, insem.at[2]),
        pltpu.make_async_copy(wy_hbm, wy_ref, insem.at[3]),
        pltpu.make_async_copy(wr_hbm, wr_ref, insem.at[4]),
    ]
    barrier = pltpu.get_barrier_semaphore()
    diagonal = [((gx + i) % DX, (gy + j) % DY) for i in (1, DX - 1) for j in (1, DY - 1)]
    known = [((gx + d) % DX, gy) for d in (1, DX - 1, 3, DX - 3, 8)] + [(gx, (gy + d) % DY) for d in (1, DY - 1, 3, DY - 3, 8)]
    for who in diagonal + known:
        pl.semaphore_signal(barrier, inc=1, device_id=who, device_id_type=MESH)
    for copy in inputs:
        copy.start()
    pl.semaphore_wait(barrier, len(diagonal) + len(known))

    copies = []
    n = 0
    for dx, dy in ((-1, -1), (-1, 1), (1, -1), (1, 1), (-1, 0), (1, 0), (0, -1), (0, 1)):
        wx = HX if dy == 0 else HX - 1
        sx = {1: (TX - wx, wx), -1: (0, wx), 0: (0, TX)}[dx]
        sy = {1: (TY - 4, 4), -1: (0, 4), 0: (0, TY)}[dy]
        tx = {1: HX - wx, -1: HX + TX, 0: HX}[dx]
        ty = {1: HY - 4, -1: HY + TY, 0: HY}[dy]
        copies.append(
            pltpu.make_async_remote_copy(
                src_ref=facies_hbm.at[pl.ds(sx[0], sx[1]), pl.ds(sy[0], sy[1])],
                dst_ref=fac.at[pl.ds(tx, sx[1]), pl.ds(ty, sy[1])],
                send_sem=hsend.at[n],
                recv_sem=hrecv.at[n],
                device_id=((gx + dx + DX) % DX, (gy + dy + DY) % DY),
                device_id_type=MESH,
            )
        )
        n += 1
    for copy in copies:
        copy.start()
    for who in known:
        pl.semaphore_signal(news, inc=1, device_id=who, device_id_type=MESH)

    for copy in inputs[1:]:
        copy.wait()
    well_x = wx_ref[...]
    well_y = wy_ref[...]
    well_r = wr_ref[...]
    sub64 = lax.broadcasted_iota(jnp.int32, (8, WELLS), 0)
    for j in range(2):
        hit_y = jnp.where(sub64 + (ay + 8 * j) == well_y, well_r, 0.0)
        for x in range(TX):
            part = jnp.where(well_x == ax + x, hit_y, 0.0)
            column = jnp.sum(part, axis=1, keepdims=True)
            rhs[x, 8 * j : 8 * j + 8, :] = source_ref[x, 8 * j : 8 * j + 8, :] + column / CELLS_Z

    last_z = flag(lane < CELLS_Z - 1)
    row_at = [ay - HY + 4 + 8 * t + sub for t in range(3)]
    row_m = [flag(inside(row - 1, GRID_Y) & inside(row, GRID_Y)) for row in row_at]
    row_p = [flag(inside(row, GRID_Y) & inside(row + 1, GRID_Y)) for row in row_at]
    same_ym = [[same_xy(row - 1, p, BLOCK_Y) for p in range(2)] for row in row_at]
    same_yp = [[same_xy(row, p, BLOCK_Y) for p in range(2)] for row in row_at]
    same_zm = [same_z(lane - 1, p) for p in range(2)]
    same_zp = [same_z(lane, p) for p in range(2)]

    def start_plane(x, _):
        gxe = ax - HX + x
        for t in range(4):
            row = ay - HY + 8 * t + sub
            for c, (i, j, k) in enumerate(COLORS):
                hit = inside(row, GRID_Y) & ((row // BLOCK_Y) % 2 == j) & ((lane // BLOCK_Z) % 2 == k)
                hitx = inside(gxe, GRID_X) & ((gxe + 2 * BLOCK_X) // BLOCK_X % 2 == i)
                va[c, x, 8 * t : 8 * t + 8, :] = flag(hit) * flag(hitx)
        return 0

    lax.fori_loop(0, EX, start_plane, 0)

    inputs[0].wait()

    half_inv = [0.5 / jnp.full((8, 128), perm_ref[f], F32) for f in range(FACIES)]
    store_at = [jnp.full((8, 128), store_ref[f], F32) for f in range(FACIES)]

    def pick(code, table):
        bits = [(code // (1 << b)) % 2 == 1 for b in range(3)]
        for b in range(3):
            table = [jnp.where(bits[b], hi, lo) for lo, hi in zip(table[::2], table[1::2])]
        return table[0]

    def lookup(tiles):
        def plane(x, _):
            for t in tiles:
                code = fac[x, 8 * t : 8 * t + 8, :]
                hperm[x, 8 * t : 8 * t + 8, :] = pick(code, half_inv)
                stor[x, 8 * t : 8 * t + 8, :] = pick(code, store_at)
            return 0

        return plane

    lax.fori_loop(HX, HX + TX, lookup((1, 2)), 0)
    for copy in copies[6:]:
        copy.wait_recv()
    lax.fori_loop(HX, HX + TX, lookup((0, 3)), 0)

    def coef_plane(x, _):
        gxe = ax - HX + x
        ok_m = flag(inside(gxe - 1, GRID_X) & inside(gxe, GRID_X))
        ok_p = flag(inside(gxe, GRID_X) & inside(gxe + 1, GRID_X))
        for t in range(3):
            r = 4 + 8 * t
            h = hperm[x, r : r + 8, :]
            txm = ok_m / (h + hperm[x - 1, r : r + 8, :])
            txp = ok_p / (h + hperm[x + 1, r : r + 8, :])
            tym = row_m[t] / (h + hperm[x, r - 1 : r + 7, :])
            typ = row_p[t] / (h + hperm[x, r + 1 : r + 9, :])
            tzp = last_z / (h + roll(h, -1))
            tzm = roll(tzp, 1)
            diag = stor[x, r : r + 8, :] + txm + txp + tym + typ + tzm + tzp
            w = RELAX / diag
            wdiag[x, r : r + 8, :] = w
            for n, value in enumerate((txm, txp, tym, typ, tzm, tzp)):
                trans[n, x, r : r + 8, :] = value
            wxm, wxp, wym, wyp, wzm, wzp = [w * v for v in (txm, txp, tym, typ, tzm, tzp)]
            a = 8 * t
            for p in range(2):
                coef[p, x, a : a + 8, :] = wxm * same_xy(gxe - 1, p, BLOCK_X)
                coef[2 + p, x, a : a + 8, :] = wxp * same_xy(gxe, p, BLOCK_X)
                coef[4 + p, x, a : a + 8, :] = wym * same_ym[t][p]
                coef[6 + p, x, a : a + 8, :] = wyp * same_yp[t][p]
                coef[8 + p, x, a : a + 8, :] = wzm * same_zm[p]
                coef[10 + p, x, a : a + 8, :] = wzp * same_zp[p]
        return 0


    def sweep(src, dst, *spans):
        def plane(x, _):
            for t in range(3):
                r, a = 4 + 8 * t, 8 * t
                k = [coef[n, x, a : a + 8, :] for n in range(12)]
                old, new = [], []
                for c, (px, py, pz) in enumerate(COLORS):
                    v = src[c, x, r : r + 8, :]
                    q = k[px] * src[c, x - 1, r : r + 8, :] + k[2 + px] * src[c, x + 1, r : r + 8, :]
                    q += k[4 + py] * src[c, x, r - 1 : r + 7, :] + k[6 + py] * src[c, x, r + 1 : r + 9, :]
                    q += k[8 + pz] * roll(v, 1) + k[10 + pz] * roll(v, -1)
                    old.append(v)
                    new.append(q)
                total = functools.reduce(jnp.add, new) - RELAX * functools.reduce(jnp.add, old)
                keep = (1.0 - RELAX) - total
                for c in range(8):
                    dst[c, x, r : r + 8, :] = new[c] + old[c] * keep
            return 0

        for span in spans:
            lax.fori_loop(*span, plane, 0, unroll=UNROLL_SWEEP)

    lax.fori_loop(5, 11, coef_plane, 0, unroll=UNROLL_COEF)
    sweep(va, vb, (5, 11))
    sweep(vb, va, (6, 10))
    sweep(va, vb, (7, 9))
    for copy in copies[:6]:
        copy.wait_recv()
    lax.fori_loop(0, HX, lookup(range(4)), 0, unroll=2)
    lax.fori_loop(HX + TX, EX, lookup(range(4)), 0, unroll=2)
    lax.fori_loop(1, 5, coef_plane, 0, unroll=UNROLL_COEF)
    lax.fori_loop(11, 15, coef_plane, 0, unroll=UNROLL_COEF)
    sweep(va, vb, (1, 5), (11, 15))
    sweep(vb, va, (2, 6), (10, 14))
    sweep(va, vb, (3, 7), (9, 13))
    basis = vb

    tile_rows = [ay + 8 * t + sub for t in range(2)]
    tile_ym = [[same_xy(row - 1, p, BLOCK_Y) for p in range(2)] for row in tile_rows]
    tile_yp = [[same_xy(row, p, BLOCK_Y) for p in range(2)] for row in tile_rows]

    def apply_plane(x, _):
        for t in range(2):
            r = HY + 8 * t
            k = [trans[n, x, r : r + 8, :] for n in range(6)]
            s = stor[x, r : r + 8, :]
            ym, yp, zm, zp = tile_ym[t], tile_yp[t], same_zm, same_zp
            for c, (px, py, pz) in enumerate(COLORS):
                v = basis[c, x, r : r + 8, :]
                q = s * v
                q += k[0] * (v - basis[c, x - 1, r : r + 8, :]) + k[1] * (v - basis[c, x + 1, r : r + 8, :])
                q += k[2] * (v - ym[py] * basis[c, x, r - 1 : r + 7, :])
                q += k[3] * (v - yp[py] * basis[c, x, r + 1 : r + 9, :])
                q += k[4] * (v - zm[pz] * roll(v, 1)) + k[5] * (v - zp[pz] * roll(v, -1))
                bv[c, x - HX, 8 * t : 8 * t + 8, :] = q
                rimy[c, x - HX, 8 * t : 8 * t + 8, :] = (
                    (ym[1 - py] - 1.0) * k[2] * basis[c, x, r - 1 : r + 7, :]
                    + (yp[1 - py] - 1.0) * k[3] * basis[c, x, r + 1 : r + 9, :]
                )
        return 0

    lax.fori_loop(HX, HX + TX, apply_plane, 0, unroll=2)

    west = lane < 64
    cut_lo = [1.0 - same_z(lane, p) for p in range(2)]
    cut_hi = [1.0 - same_z(lane - 1, p) for p in range(2)]
    turn = lane % 32 >= 16

    def rim_plane(x, acc):
        acc = list(acc)
        for t in range(2):
            r = HY + 8 * t
            tzm, tzp = trans[4, x, r : r + 8, :], trans[5, x, r : r + 8, :]
            lo = [-tzp * cut_lo[1 - p] for p in range(2)]
            hi = [-tzm * cut_hi[1 - p] for p in range(2)]
            both = -tzp * (cut_lo[0] + cut_lo[1])
            vs = [basis[c, x, r : r + 8, :] for c in range(8)]
            up = [roll(v, -1) for v in vs]
            for c, (px, py, pz) in enumerate(COLORS):
                rim[c, x - HX, 8 * t : 8 * t + 8, :] = lo[pz] * up[c] + hi[pz] * roll(vs[c], 1)
            here = [jnp.where(turn, vs[c], vs[c + 2]) for c in (0, 1, 4, 5)]
            there = [jnp.where(turn, up[c], up[c + 2]) for c in (0, 1, 4, 5)]
            first = [both * jnp.where(west, a, b) for a, b in zip(here, there)]
            second = [jnp.where(west, b, a) for a, b in zip(here, there)]
            for m in range(4):
                for n in range(4):
                    acc[4 * m + n] = acc[4 * m + n] + first[m] * second[n]
        return tuple(acc)

    zeros16 = tuple(jnp.zeros((8, 128), F32) for _ in range(16))
    acc = lax.fori_loop(HX, HX + TX, rim_plane, zeros16, unroll=2)
    for n in range(8, 12):
        wide[n] = jnp.zeros((8, 128), F32)
    corner4, edge4 = (0, 1, 4, 5), (2, 3, 6, 7)
    for m in range(4):
        for n in range(4):
            wide[8 + m, corner4[n] : corner4[n] + 1, :] = jnp.sum(acc[4 * m + n], axis=0, keepdims=True)

    parity_y = jnp.where(gy == 9, 1, 0)
    at_rim = jnp.where((gy == 5) | (gy == 9), -1.0, 0.0).astype(F32)
    top = flag(sub == 7) * at_rim

    def rim_y_plane(x, acc):
        acc = list(acc)
        t = trans[3, x, HY + 8 : HY + 16, :] * top
        here = [t * basis[c + parity_y, x, HY + 8 : HY + 16, :] for c in (0, 2, 4, 6)]
        there = [basis[c + parity_y, x, HY + 9 : HY + 17, :] for c in (0, 2, 4, 6)]
        for m in range(4):
            for n in range(4):
                acc[4 * m + n] = acc[4 * m + n] + here[m] * there[n]
        return tuple(acc)

    acc = lax.fori_loop(HX, HX + TX, rim_y_plane, zeros16, unroll=2)
    for m in range(4):
        for n in range(4):
            line = jnp.sum(acc[4 * m + n], axis=0, keepdims=True)
            wide[12 + m, 2 * n : 2 * n + 1, :] = line
            wide[12 + n, 2 * m + 1 : 2 * m + 2, :] = line

    pairs = [(a, c) for a in range(8) for c in range(a, 8)]
    for group in (pairs[:15], pairs[15:30], pairs[30:]):
        rows = sorted({a for a, _ in group})
        cols = sorted({c for _, c in group})
        last = group[-1] == (7, 7)

        def gather(x, acc, group=group, rows=rows, cols=cols, last=last):
            acc = list(acc)
            for t in range(2):
                r = HY + 8 * t
                at = slice(8 * t, 8 * t + 8)
                left = {a: basis[a, x + HX, r : r + 8, :] for a in (range(8) if last else rows)}
                right = {c: bv[c, x, at, :] for c in cols}
                own = {c: basis[c, x + HX, r : r + 8, :] for c in cols}
                over_z = {a: rim[a, x, at, :] for a in rows}
                over_y = {a: rimy[a, x, at, :] for a in rows}
                for n, (a, c) in enumerate(group):
                    acc[n] = acc[n] + left[a] * right[c]
                    if COLORS[a][2] != COLORS[c][2] and COLORS[a][1] != COLORS[c][1]:
                        acc[n] = acc[n] + own[c] * (over_z[a] + over_y[a])
                    elif COLORS[a][2] != COLORS[c][2]:
                        acc[n] = acc[n] + own[c] * over_z[a]
                    elif COLORS[a][1] != COLORS[c][1]:
                        acc[n] = acc[n] + own[c] * over_y[a]
                if last:
                    load = rhs[x, at, :]
                    for a in range(8):
                        acc[len(group) + a] = acc[len(group) + a] + left[a] * load
            return tuple(acc)

        count = len(group) + (8 if last else 0)
        acc = lax.fori_loop(0, TX, gather, tuple(jnp.zeros((8, 128), F32) for _ in range(count)), unroll=2)
        for n, (a, c) in enumerate(group):
            line = jnp.sum(acc[n], axis=0, keepdims=True)
            wide[c, a : a + 1, :] = line
            if a != c:
                wide[a, c : c + 1, :] = line
        if last:
            for a in range(8):
                at = (8, a) if a in edge4 else (9, a + 2)
                wide[at[0], at[1] : at[1] + 1, :] = jnp.sum(acc[len(group) + a], axis=0, keepdims=True)

    def ranges(places):
        total = jnp.zeros((8, 128), F32)
        for n, slot in places:
            line = wide[n]
            for step in (1, 2, 4, 8):
                line = line + roll(line, -step)
            line = jnp.where(lane % 16 == 8, line, 0.0)
            total = total + roll(line, 8 + slot)
        return total

    mine[...] = ranges(
        [(n, n) for n in range(8)] + [(8 + m, 8 + corner4[m]) for m in range(4)] + [(12 + m, 8 + edge4[m]) for m in range(4)]
    )
    pl.semaphore_wait(news, len(known))

    def exchange(src, slots, send, recv, axis):
        me = gx if axis == 0 else gy
        size = DX if axis == 0 else DY
        for d in range(1, size):
            to = ((gx + d) % DX, gy) if axis == 0 else (gx, (gy + d) % DY)
            pltpu.make_async_remote_copy(
                src_ref=src, dst_ref=slots.at[me], send_sem=send, recv_sem=recv,
                device_id=to, device_id_type=MESH,
            ).start()
        slots[me] = src[...]
        arrived = slots.at[pl.ds(0, size - 1)]
        pltpu.make_async_copy(arrived, arrived, recv).wait()
        return pltpu.make_async_copy(arrived, arrived, send)

    def tree(items):
        while len(items) > 1:
            items = [a + b for a, b in zip(items[::2], items[1::2])] + (items[-1:] if len(items) % 2 else [])
        return items[0]

    sent_x = exchange(mine, stage1, xsend, xrecv, 0)
    half[...] = tree([stage1[n] for n in range(DX)])
    sent_y = exchange(half, stage2, ysend, yrecv, 1)

    pa, pb, pc = [tree([stage2[n] for n in range(*ends)]) for ends in ((0, 6), (6, 10), (10, 16))]
    slot = lane % 16
    ly, sy = lane % 2, sub % 2
    lk, sk = lane // 2 % 2, sub // 2 % 2

    def keep(cond, value):
        return jnp.where(cond, value, 0.0)

    def rows_up(value, shift):
        return pltpu.roll(value, shift % 8, 0)

    m00, m01 = (ly == 0) & (sy == 0), (ly == 0) & (sy == 1)
    m10, m11 = (ly == 1) & (sy == 0), (ly == 1) & (sy == 1)
    qa, qb = [keep(slot % 4 == 0, roll(p, -10)) + keep(slot % 4 == 2, roll(p, -9)) for p in (pa, pb)]
    pairs_y = slot < 8
    y01 = keep(pairs_y & m00, qa) + keep(pairs_y & m11, rows_up(roll(qb, 1), 1))
    y10 = keep(pairs_y & m00, rows_up(qa, -1)) + keep(pairs_y & m11, roll(qb, 1))
    joined = [[pa + keep(m11, pb), keep(m10, pb) + y01], [keep(m01, pb) + y10, pc + keep(m00, pb)]]
    by_row = []
    for pk in range(2):
        picked = [[keep(lk == pk, joined[h][g]) for g in range(2)] for h in range(2)]
        by_row.append([
            (picked[0][g] + roll(picked[1][g], 2)) if pk == 0 else (roll(picked[0][g], -2) + picked[1][g])
            for g in range(2)
        ])

    def by_column(values, pk):
        low, high = keep(sk == pk, values[0]), keep(sk == pk, values[1])
        return low + rows_up(high, 2) if pk == 0 else rows_up(low, -2) + high

    node = [[by_column(by_row[pk], pq) for pq in range(2)] for pk in range(2)]
    loads = [pa + keep(sy == 1, pb), pc + keep(sy == 0, pb)]
    load_of = [
        keep(sk == 0, rows_up(roll(loads[0], -8), -2)) + keep(sk == 1, roll(loads[1], -8)),
        rows_up(keep(sk == 1, roll(loads[0], -7)), -2) + keep(sk == 1, roll(loads[1], -7)),
    ]
    layer = lane // 16
    even = layer % 2 == 0
    own = jnp.where(even, node[0][0] + roll(node[0][0], -16), node[1][1] + roll(node[1][1], -16))
    near_k = jnp.where(even, node[0][1], node[1][0])
    near_up = jnp.where(even, roll(node[0][1], -16), roll(node[1][0], -16))
    near_k = jnp.where(layer < 4, near_up, near_k)
    far_k = jnp.where(layer < 4, roll(node[0][0], -24), roll(node[0][0], 8))
    load_k = jnp.where(even, load_of[0] + roll(load_of[0], -16), load_of[1] + roll(load_of[1], -16))

    def ends(value, level, at):
        a, b = 16 * level + at, 16 * (7 - level) + at
        return jnp.where(west, jnp.broadcast_to(value[:, a : a + 1], (8, 128)), jnp.broadcast_to(value[:, b : b + 1], (8, 128)))

    def all_lanes(value, at):
        return jnp.broadcast_to(value[:, at : at + 1], (8, 128))

    def spread(value, k):
        return jnp.broadcast_to(value[k : k + 1, :], (8, 128))

    def eliminate(block, nexts, load, after):
        block, nexts = list(block), [list(b) for b in nexts]
        load = [spread(load, k) for k in range(8)]
        for k in range(8):
            inverse = 1.0 / spread(block[k], k)
            pivot = block[k] * inverse
            scaled = [b[k] * inverse for b in nexts]
            scaled_load = load[k] * inverse
            after([b[k] for b in nexts], scaled, scaled_load)
            for i in range(8):
                if i == k:
                    continue
                f = spread(block[i], k)
                block[i] = block[i] - f * pivot
                for b, v in zip(nexts, scaled):
                    b[i] = b[i] - f * v
                load[i] = load[i] - f * scaled_load
            block[k] = pivot
            for b, v in zip(nexts, scaled):
                b[k] = v
            load[k] = scaled_load
        return nexts, load

    diag = [[ends(own, l, i) for i in range(8)] for l in range(3)]
    one = [[ends(near_k, l, i) for i in range(8)] for l in range(3)]
    two = [[ends(far_k, l, i) for i in range(8)] for l in range(3)]
    right = [ends(load_k, l, 1) for l in range(3)]
    zero = jnp.zeros((8, 128), F32)
    d3, d4, d34 = [zero] * 8, [zero] * 8, [zero] * 8
    r3, r4 = zero, zero
    solved = []
    for level in range(3):
        def after(raw, scaled, load, level=level):
            nonlocal r3, r4
            p1, p2 = raw
            s1, s2 = scaled
            for i in range(8):
                f1, f2 = spread(p1, i), spread(p2, i)
                if level == 0:
                    diag[1][i] = diag[1][i] - f1 * s1
                    one[1][i] = one[1][i] - f1 * s2
                    diag[2][i] = diag[2][i] - f2 * s2
                elif level == 1:
                    diag[2][i] = diag[2][i] - f1 * s1
                    one[2][i] = one[2][i] - f1 * s2
                    d3[i] = d3[i] - f2 * s2
                else:
                    d3[i] = d3[i] - f1 * s1
                    d4[i] = d4[i] - f2 * s2
                    d34[i] = d34[i] - jnp.where(west, f1, f2) * jnp.where(west, s2, s1)
            if level == 0:
                right[1] = right[1] - p1 * load
                right[2] = right[2] - p2 * load
            elif level == 1:
                right[2] = right[2] - p1 * load
                r3 = r3 - p2 * load
            else:
                r3 = r3 - p1 * load
                r4 = r4 - p2 * load

        solved.append(eliminate(diag[level], [one[level], two[level]], right[level], after))

    def meet(a, b):
        value = jnp.where(west, a, b)
        return value + roll(value, 64)

    m3 = [all_lanes(own, 48 + i) + meet(d3[i], d4[i]) for i in range(8)]
    m4 = [all_lanes(own, 64 + i) + meet(d4[i], d3[i]) for i in range(8)]
    m34 = [all_lanes(near_k, 48 + i) + d34[i] + roll(d34[i], 64) for i in range(8)]
    v3 = all_lanes(load_k, 49) + meet(r3, r4)
    v4 = all_lanes(load_k, 65) + meet(r4, r3)

    def after_three(raw, scaled, load):
        nonlocal v4
        for i in range(8):
            m4[i] = m4[i] - spread(raw[0], i) * scaled[0]
        v4 = v4 - raw[0] * load

    (up3,), load3 = eliminate(m3, [m34], v3, after_three)
    _, x4 = eliminate(m4, [], v4, lambda *_: None)

    def column(items):
        value = items[0]
        for i in range(1, 8):
            value = jnp.where(sub == i, items[i], value)
        return value

    def total(value):
        return jnp.broadcast_to(jnp.sum(value, axis=0, keepdims=True), (8, 128))

    c4 = column(x4)
    x3 = [load3[i] - total(up3[i] * c4) for i in range(8)]
    c3 = column(x3)
    first, second = jnp.where(west, c3, c4), jnp.where(west, c4, c3)
    x_of = [None] * 3
    for level in (2, 1, 0):
        (n1, n2), load = solved[level]
        x_of[level] = [load[i] - total(n1[i] * first + n2[i] * second) for i in range(8)]
        first, second = column(x_of[level]), first

    node_k = [2 * ((lane + BLOCK_Z // 2) // (2 * BLOCK_Z)),
              2 * ((lane + BLOCK_Z // 2 + BLOCK_Z) // (2 * BLOCK_Z)) - 1]
    for p in range(2):
        k = node_k[p]
        at = [((k == level) & west) | ((k == 7 - level) & ~west) for level in range(3)]
        for ij in range(8):
            line = keep(k == 3, x3[ij]) + keep(k == 4, x4[ij])
            for level in range(3):
                line = jnp.where(at[level], x_of[level][ij], line)
            val[p, ij : ij + 1, :] = line[0:1, :]

    def node_row(px, py, pz, tile):
        first = tile * TY
        j = py + 2 * ((first + BLOCK_Y // 2 - BLOCK_Y * py + 4 * BLOCK_Y) // (2 * BLOCK_Y) - 2)
        j = jnp.clip(j, 0, 3)
        return val[pz, pl.ds(4 * px + j, 1), :]

    before, here, beyond = [[node_row(px, py, pz, gy + d) for px, py, pz in COLORS] for d in (-1, 0, 1)]
    for t in range(3):
        r = HY - 1 + 8 * t
        first, others = ((before, here), (here, here), (here, beyond))[t]
        weights = [jnp.where(sub == 0, a, b) for a, b in zip(first, others)]

        def prolong(x, _, r=r, weights=weights):
            prol[x, r : r + 8, :] = functools.reduce(
                jnp.add, [weights[c] * basis[c, x, r : r + 8, :] for c in range(8)]
            )
            return 0

        lax.fori_loop(HX - 1, HX + TX + 1, prolong, 0, unroll=5)

    for copy in copies:
        copy.wait_send()
    sent_x.wait()
    sent_y.wait()

    def finish(x, _):
        for t in range(2):
            r = HY + 8 * t
            v = prol[x, r : r + 8, :]
            k = [trans[n, x, r : r + 8, :] for n in range(6)]
            q = stor[x, r : r + 8, :] * v
            q += k[0] * (v - prol[x - 1, r : r + 8, :]) + k[1] * (v - prol[x + 1, r : r + 8, :])
            q += k[2] * (v - prol[x, r - 1 : r + 7, :]) + k[3] * (v - prol[x, r + 1 : r + 9, :])
            q += k[4] * (v - roll(v, 1)) + k[5] * (v - roll(v, -1))
            load = rhs[x - HX, 8 * t : 8 * t + 8, :]
            out_ref[x - HX, 8 * t : 8 * t + 8, :] = v + wdiag[x, r : r + 8, :] * (load - q)
        return 0

    lax.fori_loop(HX, HX + TX, finish, 0, unroll=2)


def per_device(facies, source, facies_perm, facies_store, well_x, well_y, well_rate):
    vmem = pl.BlockSpec(memory_space=pltpu.VMEM)
    smem = pl.BlockSpec(memory_space=pltpu.SMEM)
    hbm = pl.BlockSpec(memory_space=pltpu.HBM)
    field = pltpu.VMEM((EX, EY, 128), F32)
    colors = pltpu.VMEM((8, EX, EY, 128), F32)
    return pl.pallas_call(
        kernel,
        out_shape=jax.ShapeDtypeStruct((TX, TY, CELLS_Z), F32),
        in_specs=[hbm, hbm, smem, smem, hbm, hbm, hbm],
        out_specs=vmem,
        scratch_shapes=[
            pltpu.VMEM((EX, EY, 128), jnp.int32),
            field,
            field,
            pltpu.VMEM((12, EX, 24, 128), F32),
            pltpu.VMEM((6, EX, EY, 128), F32),
            field,
            colors,
            colors,
            pltpu.VMEM((8, TX, TY, 128), F32),
            pltpu.VMEM((8, TX, TY, 128), F32),
            pltpu.VMEM((8, TX, TY, 128), F32),
            pltpu.VMEM((TX, TY, 128), F32),
            pltpu.VMEM((16, 8, 128), F32),
            pltpu.VMEM((DX, 8, 128), F32),
            pltpu.VMEM((DY, 8, 128), F32),
            pltpu.VMEM((2, 8, 128), F32),
            field,
            pltpu.VMEM((8, 128), F32),
            pltpu.VMEM((8, 128), F32),
            pltpu.VMEM((TX, TY, 128), F32),
            pltpu.VMEM((1, WELLS), jnp.int32),
            pltpu.VMEM((1, WELLS), jnp.int32),
            pltpu.VMEM((1, WELLS), F32),
            pltpu.SemaphoreType.DMA((5,)),
            pltpu.SemaphoreType.DMA((8,)),
            pltpu.SemaphoreType.DMA((8,)),
            pltpu.SemaphoreType.DMA,
            pltpu.SemaphoreType.DMA,
            pltpu.SemaphoreType.DMA,
            pltpu.SemaphoreType.DMA,
            pltpu.SemaphoreType.REGULAR,
        ],
        compiler_params=pltpu.CompilerParams(
            collective_id=0, has_side_effects=True, vmem_limit_bytes=40 * 1024 * 1024
        ),
    )(
        facies, source, facies_perm, facies_store,
        well_x.reshape(1, WELLS), well_y.reshape(1, WELLS), well_rate.reshape(1, WELLS),
    )


def solution(mesh):
    in_specs = (P("gx", "gy", None), P("gx", "gy", None), P(), P(), P(), P(), P())
    return jax.shard_map(
        per_device, mesh=mesh, in_specs=in_specs, out_specs=P("gx", "gy", None), check_vma=False
    )
```

```python
import functools

import jax
import jax.numpy as jnp
from jax import lax
from jax.experimental import pallas as pl
from jax.experimental.pallas import tpu as pltpu
from jax.sharding import PartitionSpec as P

GRID_X, GRID_Y, CELLS_Z = 128, 256, 128
BLOCK_X, BLOCK_Y, BLOCK_Z = 64, 64, 16
FACIES = 8
WELLS = 64
RELAX = 2.0 / 3.0

TX, TY = 8, 16
HX, HY = 4, 8
EX, EY = TX + 2 * HX, TY + 2 * HY
DX, DY = 16, 16
MESH = pl.DeviceIdType.MESH
UNROLL_SWEEP, UNROLL_COEF = True, True
F32 = jnp.float32

COLORS = [(c >> 2 & 1, c & 1, c >> 1 & 1) for c in range(8)]


def roll(value, shift):
    return pltpu.roll(value, shift % 128, 1)


def iota(dim):
    return lax.broadcasted_iota(jnp.int32, (8, 128), dim)


def flag(cond):
    return jnp.where(cond, 1.0, 0.0).astype(F32)


def same_xy(coord, parity, block):
    return flag((coord + 1 + block // 2 - block * parity + 4 * block) % (2 * block) != 0)


def same_z(coord, parity):
    return flag((coord + 1 + BLOCK_Z // 2 - BLOCK_Z * parity + 2 * BLOCK_Z) % (2 * BLOCK_Z) != 0)


def inside(coord, total):
    return (coord >= 0) & (coord < total)


def kernel(
    facies_hbm, source_hbm, perm_ref, store_ref, wx_hbm, wy_hbm, wr_hbm, out_ref,
    fac, hperm, stor, coef, trans, wdiag, va, vb, bv, rim, rimy, rhs, wide, stage1, stage2, val, prol,
    mine, half, source_ref, wx_ref, wy_ref, wr_ref,
    insem, hsend, hrecv, xsend, xrecv, ysend, yrecv, news,
):
    gx = lax.axis_index("gx")
    gy = lax.axis_index("gy")
    ax, ay = gx * TX, gy * TY
    lane, sub = iota(1), iota(0)

    inputs = [
        pltpu.make_async_copy(facies_hbm, fac.at[pl.ds(HX, TX), pl.ds(HY, TY)], insem.at[0]),
        pltpu.make_async_copy(source_hbm, source_ref, insem.at[1]),
        pltpu.make_async_copy(wx_hbm, wx_ref, insem.at[2]),
        pltpu.make_async_copy(wy_hbm, wy_ref, insem.at[3]),
        pltpu.make_async_copy(wr_hbm, wr_ref, insem.at[4]),
    ]
    barrier = pltpu.get_barrier_semaphore()
    diagonal = [((gx + i) % DX, (gy + j) % DY) for i in (1, DX - 1) for j in (1, DY - 1)]
    known = [((gx + d) % DX, gy) for d in (1, DX - 1, 3, DX - 3, 8)] + [(gx, (gy + d) % DY) for d in (1, DY - 1, 3, DY - 3, 8)]
    for who in diagonal + known:
        pl.semaphore_signal(barrier, inc=1, device_id=who, device_id_type=MESH)
    for copy in inputs:
        copy.start()
    pl.semaphore_wait(barrier, len(diagonal) + len(known))

    copies = []
    n = 0
    for dx, dy in ((-1, -1), (-1, 1), (1, -1), (1, 1), (-1, 0), (1, 0), (0, -1), (0, 1)):
        wx = HX if dy == 0 else HX - 1
        sx = {1: (TX - wx, wx), -1: (0, wx), 0: (0, TX)}[dx]
        sy = {1: (TY - 4, 4), -1: (0, 4), 0: (0, TY)}[dy]
        tx = {1: HX - wx, -1: HX + TX, 0: HX}[dx]
        ty = {1: HY - 4, -1: HY + TY, 0: HY}[dy]
        copies.append(
            pltpu.make_async_remote_copy(
                src_ref=facies_hbm.at[pl.ds(sx[0], sx[1]), pl.ds(sy[0], sy[1])],
                dst_ref=fac.at[pl.ds(tx, sx[1]), pl.ds(ty, sy[1])],
                send_sem=hsend.at[n],
                recv_sem=hrecv.at[n],
                device_id=((gx + dx + DX) % DX, (gy + dy + DY) % DY),
                device_id_type=MESH,
            )
        )
        n += 1
    for copy in copies:
        copy.start()
    for who in known:
        pl.semaphore_signal(news, inc=1, device_id=who, device_id_type=MESH)

    for copy in inputs[1:]:
        copy.wait()
    well_x = wx_ref[...]
    well_y = wy_ref[...]
    well_r = wr_ref[...]
    sub64 = lax.broadcasted_iota(jnp.int32, (8, WELLS), 0)
    for j in range(2):
        hit_y = jnp.where(sub64 + (ay + 8 * j) == well_y, well_r, 0.0)
        for x in range(TX):
            part = jnp.where(well_x == ax + x, hit_y, 0.0)
            column = jnp.sum(part, axis=1, keepdims=True)
            rhs[x, 8 * j : 8 * j + 8, :] = source_ref[x, 8 * j : 8 * j + 8, :] + column / CELLS_Z

    last_z = flag(lane < CELLS_Z - 1)
    row_at = [ay - HY + 4 + 8 * t + sub for t in range(3)]
    row_m = [flag(inside(row - 1, GRID_Y) & inside(row, GRID_Y)) for row in row_at]
    row_p = [flag(inside(row, GRID_Y) & inside(row + 1, GRID_Y)) for row in row_at]
    same_ym = [[same_xy(row - 1, p, BLOCK_Y) for p in range(2)] for row in row_at]
    same_yp = [[same_xy(row, p, BLOCK_Y) for p in range(2)] for row in row_at]
    same_zm = [same_z(lane - 1, p) for p in range(2)]
    same_zp = [same_z(lane, p) for p in range(2)]

    def start_plane(x, _):
        gxe = ax - HX + x
        for t in range(4):
            row = ay - HY + 8 * t + sub
            for c, (i, j, k) in enumerate(COLORS):
                hit = inside(row, GRID_Y) & ((row // BLOCK_Y) % 2 == j) & ((lane // BLOCK_Z) % 2 == k)
                hitx = inside(gxe, GRID_X) & ((gxe + 2 * BLOCK_X) // BLOCK_X % 2 == i)
                va[c, x, 8 * t : 8 * t + 8, :] = flag(hit) * flag(hitx)
        return 0

    lax.fori_loop(0, EX, start_plane, 0)

    inputs[0].wait()

    half_inv = [0.5 / jnp.full((8, 128), perm_ref[f], F32) for f in range(FACIES)]
    store_at = [jnp.full((8, 128), store_ref[f], F32) for f in range(FACIES)]

    def pick(code, table):
        bits = [(code // (1 << b)) % 2 == 1 for b in range(3)]
        for b in range(3):
            table = [jnp.where(bits[b], hi, lo) for lo, hi in zip(table[::2], table[1::2])]
        return table[0]

    def lookup(tiles):
        def plane(x, _):
            for t in tiles:
                code = fac[x, 8 * t : 8 * t + 8, :]
                hperm[x, 8 * t : 8 * t + 8, :] = pick(code, half_inv)
                stor[x, 8 * t : 8 * t + 8, :] = pick(code, store_at)
            return 0

        return plane

    lax.fori_loop(HX, HX + TX, lookup((1, 2)), 0, unroll=2)
    for copy in copies[6:]:
        copy.wait_recv()
    lax.fori_loop(HX, HX + TX, lookup((0, 3)), 0, unroll=True)

    def coef_plane(x, _):
        gxe = ax - HX + x
        ok_m = flag(inside(gxe - 1, GRID_X) & inside(gxe, GRID_X))
        ok_p = flag(inside(gxe, GRID_X) & inside(gxe + 1, GRID_X))
        for t in range(3):
            r = 4 + 8 * t
            h = hperm[x, r : r + 8, :]
            txm = ok_m / (h + hperm[x - 1, r : r + 8, :])
            txp = ok_p / (h + hperm[x + 1, r : r + 8, :])
            tym = row_m[t] / (h + hperm[x, r - 1 : r + 7, :])
            typ = row_p[t] / (h + hperm[x, r + 1 : r + 9, :])
            tzp = last_z / (h + roll(h, -1))
            tzm = roll(tzp, 1)
            diag = stor[x, r : r + 8, :] + txm + txp + tym + typ + tzm + tzp
            w = RELAX / diag
            wdiag[x, r : r + 8, :] = w
            for n, value in enumerate((txm, txp, tym, typ, tzm, tzp)):
                trans[n, x, r : r + 8, :] = value
            wxm, wxp, wym, wyp, wzm, wzp = [w * v for v in (txm, txp, tym, typ, tzm, tzp)]
            a = 8 * t
            for p in range(2):
                coef[p, x, a : a + 8, :] = wxm * same_xy(gxe - 1, p, BLOCK_X)
                coef[2 + p, x, a : a + 8, :] = wxp * same_xy(gxe, p, BLOCK_X)
                coef[4 + p, x, a : a + 8, :] = wym * same_ym[t][p]
                coef[6 + p, x, a : a + 8, :] = wyp * same_yp[t][p]
                coef[8 + p, x, a : a + 8, :] = wzm * same_zm[p]
                coef[10 + p, x, a : a + 8, :] = wzp * same_zp[p]
        return 0


    def sweep(src, dst, *spans):
        def plane(x, _):
            for t in range(3):
                r, a = 4 + 8 * t, 8 * t
                k = [coef[n, x, a : a + 8, :] for n in range(12)]
                old, new = [], []
                for c, (px, py, pz) in enumerate(COLORS):
                    v = src[c, x, r : r + 8, :]
                    q = k[px] * src[c, x - 1, r : r + 8, :] + k[2 + px] * src[c, x + 1, r : r + 8, :]
                    q += k[4 + py] * src[c, x, r - 1 : r + 7, :] + k[6 + py] * src[c, x, r + 1 : r + 9, :]
                    q += k[8 + pz] * roll(v, 1) + k[10 + pz] * roll(v, -1)
                    old.append(v)
                    new.append(q)
                total = functools.reduce(jnp.add, new) - RELAX * functools.reduce(jnp.add, old)
                keep = (1.0 - RELAX) - total
                for c in range(8):
                    dst[c, x, r : r + 8, :] = new[c] + old[c] * keep
            return 0

        for span in spans:
            lax.fori_loop(*span, plane, 0, unroll=UNROLL_SWEEP)

    lax.fori_loop(5, 11, coef_plane, 0, unroll=UNROLL_COEF)
    sweep(va, vb, (5, 11))
    sweep(vb, va, (6, 10))
    sweep(va, vb, (7, 9))
    for copy in copies[:6]:
        copy.wait_recv()
    lax.fori_loop(0, HX, lookup(range(4)), 0, unroll=True)
    lax.fori_loop(HX + TX, EX, lookup(range(4)), 0, unroll=True)
    lax.fori_loop(1, 5, coef_plane, 0, unroll=UNROLL_COEF)
    lax.fori_loop(11, 15, coef_plane, 0, unroll=UNROLL_COEF)
    sweep(va, vb, (1, 5), (11, 15))
    sweep(vb, va, (2, 6), (10, 14))
    sweep(va, vb, (3, 7), (9, 13))
    basis = vb

    tile_rows = [ay + 8 * t + sub for t in range(2)]
    tile_ym = [[same_xy(row - 1, p, BLOCK_Y) for p in range(2)] for row in tile_rows]
    tile_yp = [[same_xy(row, p, BLOCK_Y) for p in range(2)] for row in tile_rows]

    def apply_plane(x, _):
        for t in range(2):
            r = HY + 8 * t
            k = [trans[n, x, r : r + 8, :] for n in range(6)]
            s = stor[x, r : r + 8, :]
            ym, yp, zm, zp = tile_ym[t], tile_yp[t], same_zm, same_zp
            for c, (px, py, pz) in enumerate(COLORS):
                v = basis[c, x, r : r + 8, :]
                q = s * v
                q += k[0] * (v - basis[c, x - 1, r : r + 8, :]) + k[1] * (v - basis[c, x + 1, r : r + 8, :])
                q += k[2] * (v - ym[py] * basis[c, x, r - 1 : r + 7, :])
                q += k[3] * (v - yp[py] * basis[c, x, r + 1 : r + 9, :])
                q += k[4] * (v - zm[pz] * roll(v, 1)) + k[5] * (v - zp[pz] * roll(v, -1))
                bv[c, x - HX, 8 * t : 8 * t + 8, :] = q
                rimy[c, x - HX, 8 * t : 8 * t + 8, :] = (
                    (ym[1 - py] - 1.0) * k[2] * basis[c, x, r - 1 : r + 7, :]
                    + (yp[1 - py] - 1.0) * k[3] * basis[c, x, r + 1 : r + 9, :]
                )
        return 0

    lax.fori_loop(HX, HX + TX, apply_plane, 0, unroll=True)

    west = lane < 64
    cut_lo = [1.0 - same_z(lane, p) for p in range(2)]
    cut_hi = [1.0 - same_z(lane - 1, p) for p in range(2)]
    turn = lane % 32 >= 16

    def rim_plane(x, acc):
        acc = list(acc)
        for t in range(2):
            r = HY + 8 * t
            tzm, tzp = trans[4, x, r : r + 8, :], trans[5, x, r : r + 8, :]
            lo = [-tzp * cut_lo[1 - p] for p in range(2)]
            hi = [-tzm * cut_hi[1 - p] for p in range(2)]
            both = -tzp * (cut_lo[0] + cut_lo[1])
            vs = [basis[c, x, r : r + 8, :] for c in range(8)]
            up = [roll(v, -1) for v in vs]
            for c, (px, py, pz) in enumerate(COLORS):
                rim[c, x - HX, 8 * t : 8 * t + 8, :] = lo[pz] * up[c] + hi[pz] * roll(vs[c], 1)
            here = [jnp.where(turn, vs[c], vs[c + 2]) for c in (0, 1, 4, 5)]
            there = [jnp.where(turn, up[c], up[c + 2]) for c in (0, 1, 4, 5)]
            first = [both * jnp.where(west, a, b) for a, b in zip(here, there)]
            second = [jnp.where(west, b, a) for a, b in zip(here, there)]
            for m in range(4):
                for n in range(4):
                    acc[4 * m + n] = acc[4 * m + n] + first[m] * second[n]
        return tuple(acc)

    zeros16 = tuple(jnp.zeros((8, 128), F32) for _ in range(16))
    acc = lax.fori_loop(HX, HX + TX, rim_plane, zeros16, unroll=True)
    for n in range(8, 12):
        wide[n] = jnp.zeros((8, 128), F32)
    corner4, edge4 = (0, 1, 4, 5), (2, 3, 6, 7)
    for m in range(4):
        for n in range(4):
            wide[8 + m, corner4[n] : corner4[n] + 1, :] = jnp.sum(acc[4 * m + n], axis=0, keepdims=True)

    parity_y = jnp.where(gy == 9, 1, 0)
    at_rim = jnp.where((gy == 5) | (gy == 9), -1.0, 0.0).astype(F32)
    top = flag(sub == 7) * at_rim

    def rim_y_plane(x, acc):
        acc = list(acc)
        t = trans[3, x, HY + 8 : HY + 16, :] * top
        here = [t * basis[c + parity_y, x, HY + 8 : HY + 16, :] for c in (0, 2, 4, 6)]
        there = [basis[c + parity_y, x, HY + 9 : HY + 17, :] for c in (0, 2, 4, 6)]
        for m in range(4):
            for n in range(4):
                acc[4 * m + n] = acc[4 * m + n] + here[m] * there[n]
        return tuple(acc)

    acc = lax.fori_loop(HX, HX + TX, rim_y_plane, zeros16, unroll=True)
    for m in range(4):
        for n in range(4):
            line = jnp.sum(acc[4 * m + n], axis=0, keepdims=True)
            wide[12 + m, 2 * n : 2 * n + 1, :] = line
            wide[12 + n, 2 * m + 1 : 2 * m + 2, :] = line

    pairs = [(a, c) for a in range(8) for c in range(a, 8)]
    for group in (pairs[:15], pairs[15:30], pairs[30:]):
        rows = sorted({a for a, _ in group})
        cols = sorted({c for _, c in group})
        last = group[-1] == (7, 7)

        def gather(x, acc, group=group, rows=rows, cols=cols, last=last):
            acc = list(acc)
            for t in range(2):
                r = HY + 8 * t
                at = slice(8 * t, 8 * t + 8)
                left = {a: basis[a, x + HX, r : r + 8, :] for a in (range(8) if last else rows)}
                right = {c: bv[c, x, at, :] for c in cols}
                own = {c: basis[c, x + HX, r : r + 8, :] for c in cols}
                over_z = {a: rim[a, x, at, :] for a in rows}
                over_y = {a: rimy[a, x, at, :] for a in rows}
                for n, (a, c) in enumerate(group):
                    acc[n] = acc[n] + left[a] * right[c]
                    if COLORS[a][2] != COLORS[c][2] and COLORS[a][1] != COLORS[c][1]:
                        acc[n] = acc[n] + own[c] * (over_z[a] + over_y[a])
                    elif COLORS[a][2] != COLORS[c][2]:
                        acc[n] = acc[n] + own[c] * over_z[a]
                    elif COLORS[a][1] != COLORS[c][1]:
                        acc[n] = acc[n] + own[c] * over_y[a]
                if last:
                    load = rhs[x, at, :]
                    for a in range(8):
                        acc[len(group) + a] = acc[len(group) + a] + left[a] * load
            return tuple(acc)

        count = len(group) + (8 if last else 0)
        acc = lax.fori_loop(0, TX, gather, tuple(jnp.zeros((8, 128), F32) for _ in range(count)), unroll=True)
        for n, (a, c) in enumerate(group):
            line = jnp.sum(acc[n], axis=0, keepdims=True)
            wide[c, a : a + 1, :] = line
            if a != c:
                wide[a, c : c + 1, :] = line
        if last:
            for a in range(8):
                at = (8, a) if a in edge4 else (9, a + 2)
                wide[at[0], at[1] : at[1] + 1, :] = jnp.sum(acc[len(group) + a], axis=0, keepdims=True)

    def ranges(places):
        total = jnp.zeros((8, 128), F32)
        for n, slot in places:
            line = wide[n]
            for step in (1, 2, 4, 8):
                line = line + roll(line, -step)
            line = jnp.where(lane % 16 == 8, line, 0.0)
            total = total + roll(line, 8 + slot)
        return total

    mine[...] = ranges(
        [(n, n) for n in range(8)] + [(8 + m, 8 + corner4[m]) for m in range(4)] + [(12 + m, 8 + edge4[m]) for m in range(4)]
    )
    pl.semaphore_wait(news, len(known))

    def exchange(src, slots, send, recv, axis):
        me = gx if axis == 0 else gy
        size = DX if axis == 0 else DY
        for d in range(1, size):
            to = ((gx + d) % DX, gy) if axis == 0 else (gx, (gy + d) % DY)
            pltpu.make_async_remote_copy(
                src_ref=src, dst_ref=slots.at[me], send_sem=send, recv_sem=recv,
                device_id=to, device_id_type=MESH,
            ).start()
        slots[me] = src[...]
        arrived = slots.at[pl.ds(0, size - 1)]
        pltpu.make_async_copy(arrived, arrived, recv).wait()
        return pltpu.make_async_copy(arrived, arrived, send)

    def tree(items):
        while len(items) > 1:
            items = [a + b for a, b in zip(items[::2], items[1::2])] + (items[-1:] if len(items) % 2 else [])
        return items[0]

    sent_x = exchange(mine, stage1, xsend, xrecv, 0)
    half[...] = tree([stage1[n] for n in range(DX)])
    sent_y = exchange(half, stage2, ysend, yrecv, 1)

    pa, pb, pc = [tree([stage2[n] for n in range(*ends)]) for ends in ((0, 6), (6, 10), (10, 16))]
    slot = lane % 16
    ly, sy = lane % 2, sub % 2
    lk, sk = lane // 2 % 2, sub // 2 % 2

    def keep(cond, value):
        return jnp.where(cond, value, 0.0)

    def rows_up(value, shift):
        return pltpu.roll(value, shift % 8, 0)

    m00, m01 = (ly == 0) & (sy == 0), (ly == 0) & (sy == 1)
    m10, m11 = (ly == 1) & (sy == 0), (ly == 1) & (sy == 1)
    qa, qb = [keep(slot % 4 == 0, roll(p, -10)) + keep(slot % 4 == 2, roll(p, -9)) for p in (pa, pb)]
    pairs_y = slot < 8
    y01 = keep(pairs_y & m00, qa) + keep(pairs_y & m11, rows_up(roll(qb, 1), 1))
    y10 = keep(pairs_y & m00, rows_up(qa, -1)) + keep(pairs_y & m11, roll(qb, 1))
    joined = [[pa + keep(m11, pb), keep(m10, pb) + y01], [keep(m01, pb) + y10, pc + keep(m00, pb)]]
    by_row = []
    for pk in range(2):
        picked = [[keep(lk == pk, joined[h][g]) for g in range(2)] for h in range(2)]
        by_row.append([
            (picked[0][g] + roll(picked[1][g], 2)) if pk == 0 else (roll(picked[0][g], -2) + picked[1][g])
            for g in range(2)
        ])

    def by_column(values, pk):
        low, high = keep(sk == pk, values[0]), keep(sk == pk, values[1])
        return low + rows_up(high, 2) if pk == 0 else rows_up(low, -2) + high

    node = [[by_column(by_row[pk], pq) for pq in range(2)] for pk in range(2)]
    loads = [pa + keep(sy == 1, pb), pc + keep(sy == 0, pb)]
    load_of = [
        keep(sk == 0, rows_up(roll(loads[0], -8), -2)) + keep(sk == 1, roll(loads[1], -8)),
        rows_up(keep(sk == 1, roll(loads[0], -7)), -2) + keep(sk == 1, roll(loads[1], -7)),
    ]
    layer = lane // 16
    even = layer % 2 == 0
    own = jnp.where(even, node[0][0] + roll(node[0][0], -16), node[1][1] + roll(node[1][1], -16))
    near_k = jnp.where(even, node[0][1], node[1][0])
    near_up = jnp.where(even, roll(node[0][1], -16), roll(node[1][0], -16))
    near_k = jnp.where(layer < 4, near_up, near_k)
    far_k = jnp.where(layer < 4, roll(node[0][0], -24), roll(node[0][0], 8))
    load_k = jnp.where(even, load_of[0] + roll(load_of[0], -16), load_of[1] + roll(load_of[1], -16))

    def ends(value, level, at):
        a, b = 16 * level + at, 16 * (7 - level) + at
        return jnp.where(west, jnp.broadcast_to(value[:, a : a + 1], (8, 128)), jnp.broadcast_to(value[:, b : b + 1], (8, 128)))

    def all_lanes(value, at):
        return jnp.broadcast_to(value[:, at : at + 1], (8, 128))

    def spread(value, k):
        return jnp.broadcast_to(value[k : k + 1, :], (8, 128))

    def eliminate(block, nexts, load, after):
        block, nexts = list(block), [list(b) for b in nexts]
        load = [spread(load, k) for k in range(8)]
        for k in range(8):
            inverse = 1.0 / spread(block[k], k)
            pivot = block[k] * inverse
            scaled = [b[k] * inverse for b in nexts]
            scaled_load = load[k] * inverse
            after([b[k] for b in nexts], scaled, scaled_load)
            for i in range(8):
                if i == k:
                    continue
                f = spread(block[i], k)
                block[i] = block[i] - f * pivot
                for b, v in zip(nexts, scaled):
                    b[i] = b[i] - f * v
                load[i] = load[i] - f * scaled_load
            block[k] = pivot
            for b, v in zip(nexts, scaled):
                b[k] = v
            load[k] = scaled_load
        return nexts, load

    diag = [[ends(own, l, i) for i in range(8)] for l in range(3)]
    one = [[ends(near_k, l, i) for i in range(8)] for l in range(3)]
    two = [[ends(far_k, l, i) for i in range(8)] for l in range(3)]
    right = [ends(load_k, l, 1) for l in range(3)]
    zero = jnp.zeros((8, 128), F32)
    d3, d4, d34 = [zero] * 8, [zero] * 8, [zero] * 8
    r3, r4 = zero, zero
    solved = []
    for level in range(3):
        def after(raw, scaled, load, level=level):
            nonlocal r3, r4
            p1, p2 = raw
            s1, s2 = scaled
            for i in range(8):
                f1, f2 = spread(p1, i), spread(p2, i)
                if level == 0:
                    diag[1][i] = diag[1][i] - f1 * s1
                    one[1][i] = one[1][i] - f1 * s2
                    diag[2][i] = diag[2][i] - f2 * s2
                elif level == 1:
                    diag[2][i] = diag[2][i] - f1 * s1
                    one[2][i] = one[2][i] - f1 * s2
                    d3[i] = d3[i] - f2 * s2
                else:
                    d3[i] = d3[i] - f1 * s1
                    d4[i] = d4[i] - f2 * s2
                    d34[i] = d34[i] - jnp.where(west, f1, f2) * jnp.where(west, s2, s1)
            if level == 0:
                right[1] = right[1] - p1 * load
                right[2] = right[2] - p2 * load
            elif level == 1:
                right[2] = right[2] - p1 * load
                r3 = r3 - p2 * load
            else:
                r3 = r3 - p1 * load
                r4 = r4 - p2 * load

        solved.append(eliminate(diag[level], [one[level], two[level]], right[level], after))

    def meet(a, b):
        value = jnp.where(west, a, b)
        return value + roll(value, 64)

    m3 = [all_lanes(own, 48 + i) + meet(d3[i], d4[i]) for i in range(8)]
    m4 = [all_lanes(own, 64 + i) + meet(d4[i], d3[i]) for i in range(8)]
    m34 = [all_lanes(near_k, 48 + i) + d34[i] + roll(d34[i], 64) for i in range(8)]
    v3 = all_lanes(load_k, 49) + meet(r3, r4)
    v4 = all_lanes(load_k, 65) + meet(r4, r3)

    def after_three(raw, scaled, load):
        nonlocal v4
        for i in range(8):
            m4[i] = m4[i] - spread(raw[0], i) * scaled[0]
        v4 = v4 - raw[0] * load

    (up3,), load3 = eliminate(m3, [m34], v3, after_three)
    _, x4 = eliminate(m4, [], v4, lambda *_: None)

    def column(items):
        value = items[0]
        for i in range(1, 8):
            value = jnp.where(sub == i, items[i], value)
        return value

    def total(value):
        return jnp.broadcast_to(jnp.sum(value, axis=0, keepdims=True), (8, 128))

    c4 = column(x4)
    x3 = [load3[i] - total(up3[i] * c4) for i in range(8)]
    c3 = column(x3)
    first, second = jnp.where(west, c3, c4), jnp.where(west, c4, c3)
    x_of = [None] * 3
    for level in (2, 1, 0):
        (n1, n2), load = solved[level]
        x_of[level] = [load[i] - total(n1[i] * first + n2[i] * second) for i in range(8)]
        first, second = column(x_of[level]), first

    node_k = [2 * ((lane + BLOCK_Z // 2) // (2 * BLOCK_Z)),
              2 * ((lane + BLOCK_Z // 2 + BLOCK_Z) // (2 * BLOCK_Z)) - 1]
    for p in range(2):
        k = node_k[p]
        at = [((k == level) & west) | ((k == 7 - level) & ~west) for level in range(3)]
        for ij in range(8):
            line = keep(k == 3, x3[ij]) + keep(k == 4, x4[ij])
            for level in range(3):
                line = jnp.where(at[level], x_of[level][ij], line)
            val[p, ij : ij + 1, :] = line[0:1, :]

    def node_row(px, py, pz, tile):
        first = tile * TY
        j = py + 2 * ((first + BLOCK_Y // 2 - BLOCK_Y * py + 4 * BLOCK_Y) // (2 * BLOCK_Y) - 2)
        j = jnp.clip(j, 0, 3)
        return val[pz, pl.ds(4 * px + j, 1), :]

    before, here, beyond = [[node_row(px, py, pz, gy + d) for px, py, pz in COLORS] for d in (-1, 0, 1)]
    for t in range(3):
        r = HY - 1 + 8 * t
        first, others = ((before, here), (here, here), (here, beyond))[t]
        weights = [jnp.where(sub == 0, a, b) for a, b in zip(first, others)]

        def prolong(x, _, r=r, weights=weights):
            prol[x, r : r + 8, :] = functools.reduce(
                jnp.add, [weights[c] * basis[c, x, r : r + 8, :] for c in range(8)]
            )
            return 0

        lax.fori_loop(HX - 1, HX + TX + 1, prolong, 0, unroll=5)

    for copy in copies:
        copy.wait_send()
    sent_x.wait()
    sent_y.wait()

    def finish(x, _):
        for t in range(2):
            r = HY + 8 * t
            v = prol[x, r : r + 8, :]
            k = [trans[n, x, r : r + 8, :] for n in range(6)]
            q = stor[x, r : r + 8, :] * v
            q += k[0] * (v - prol[x - 1, r : r + 8, :]) + k[1] * (v - prol[x + 1, r : r + 8, :])
            q += k[2] * (v - prol[x, r - 1 : r + 7, :]) + k[3] * (v - prol[x, r + 1 : r + 9, :])
            q += k[4] * (v - roll(v, 1)) + k[5] * (v - roll(v, -1))
            load = rhs[x - HX, 8 * t : 8 * t + 8, :]
            out_ref[x - HX, 8 * t : 8 * t + 8, :] = v + wdiag[x, r : r + 8, :] * (load - q)
        return 0

    lax.fori_loop(HX, HX + TX, finish, 0, unroll=True)


def per_device(facies, source, facies_perm, facies_store, well_x, well_y, well_rate):
    vmem = pl.BlockSpec(memory_space=pltpu.VMEM)
    smem = pl.BlockSpec(memory_space=pltpu.SMEM)
    hbm = pl.BlockSpec(memory_space=pltpu.HBM)
    field = pltpu.VMEM((EX, EY, 128), F32)
    colors = pltpu.VMEM((8, EX, EY, 128), F32)
    return pl.pallas_call(
        kernel,
        out_shape=jax.ShapeDtypeStruct((TX, TY, CELLS_Z), F32),
        in_specs=[hbm, hbm, smem, smem, hbm, hbm, hbm],
        out_specs=vmem,
        scratch_shapes=[
            pltpu.VMEM((EX, EY, 128), jnp.int32),
            field,
            field,
            pltpu.VMEM((12, EX, 24, 128), F32),
            pltpu.VMEM((6, EX, EY, 128), F32),
            field,
            colors,
            colors,
            pltpu.VMEM((8, TX, TY, 128), F32),
            pltpu.VMEM((8, TX, TY, 128), F32),
            pltpu.VMEM((8, TX, TY, 128), F32),
            pltpu.VMEM((TX, TY, 128), F32),
            pltpu.VMEM((16, 8, 128), F32),
            pltpu.VMEM((DX, 8, 128), F32),
            pltpu.VMEM((DY, 8, 128), F32),
            pltpu.VMEM((2, 8, 128), F32),
            field,
            pltpu.VMEM((8, 128), F32),
            pltpu.VMEM((8, 128), F32),
            pltpu.VMEM((TX, TY, 128), F32),
            pltpu.VMEM((1, WELLS), jnp.int32),
            pltpu.VMEM((1, WELLS), jnp.int32),
            pltpu.VMEM((1, WELLS), F32),
            pltpu.SemaphoreType.DMA((5,)),
            pltpu.SemaphoreType.DMA((8,)),
            pltpu.SemaphoreType.DMA((8,)),
            pltpu.SemaphoreType.DMA,
            pltpu.SemaphoreType.DMA,
            pltpu.SemaphoreType.DMA,
            pltpu.SemaphoreType.DMA,
            pltpu.SemaphoreType.REGULAR,
        ],
        compiler_params=pltpu.CompilerParams(
            collective_id=0, has_side_effects=True, vmem_limit_bytes=40 * 1024 * 1024
        ),
    )(
        facies, source, facies_perm, facies_store,
        well_x.reshape(1, WELLS), well_y.reshape(1, WELLS), well_rate.reshape(1, WELLS),
    )


def solution(mesh):
    in_specs = (P("gx", "gy", None), P("gx", "gy", None), P(), P(), P(), P(), P())
    return jax.shard_map(
        per_device, mesh=mesh, in_specs=in_specs, out_specs=P("gx", "gy", None), check_vma=False
    )
```

```python
import functools

import jax
import jax.numpy as jnp
from jax import lax
from jax.experimental import pallas as pl
from jax.experimental.pallas import tpu as pltpu
from jax.sharding import PartitionSpec as P

GRID_X, GRID_Y, CELLS_Z = 128, 256, 128
BLOCK_X, BLOCK_Y, BLOCK_Z = 64, 64, 16
FACIES = 8
WELLS = 64
RELAX = 2.0 / 3.0

TX, TY = 8, 16
HX, HY = 4, 8
EX, EY = TX + 2 * HX, TY + 2 * HY
DX, DY = 16, 16
MESH = pl.DeviceIdType.MESH
UNROLL_SWEEP, UNROLL_COEF = True, True
F32 = jnp.float32

COLORS = [(c >> 2 & 1, c & 1, c >> 1 & 1) for c in range(8)]


def roll(value, shift):
    return pltpu.roll(value, shift % 128, 1)


def iota(dim):
    return lax.broadcasted_iota(jnp.int32, (8, 128), dim)


def flag(cond):
    return jnp.where(cond, 1.0, 0.0).astype(F32)


def same_xy(coord, parity, block):
    return flag((coord + 1 + block // 2 - block * parity + 4 * block) % (2 * block) != 0)


def same_z(coord, parity):
    return flag((coord + 1 + BLOCK_Z // 2 - BLOCK_Z * parity + 2 * BLOCK_Z) % (2 * BLOCK_Z) != 0)


def inside(coord, total):
    return (coord >= 0) & (coord < total)


def kernel(
    facies_hbm, source_hbm, perm_ref, store_ref, wx_hbm, wy_hbm, wr_hbm, out_ref,
    fac, hperm, stor, coef, trans, wdiag, va, vb, bv, rim, rimy, rhs, wide, stage1, stage2, val, prol,
    mine, half, source_ref, wx_ref, wy_ref, wr_ref,
    insem, hsend, hrecv, xsend, xrecv, ysend, yrecv, news,
):
    gx = lax.axis_index("gx")
    gy = lax.axis_index("gy")
    ax, ay = gx * TX, gy * TY
    lane, sub = iota(1), iota(0)

    inputs = [
        pltpu.make_async_copy(facies_hbm, fac.at[pl.ds(HX, TX), pl.ds(HY, TY)], insem.at[0]),
        pltpu.make_async_copy(source_hbm, source_ref, insem.at[1]),
        pltpu.make_async_copy(wx_hbm, wx_ref, insem.at[2]),
        pltpu.make_async_copy(wy_hbm, wy_ref, insem.at[3]),
        pltpu.make_async_copy(wr_hbm, wr_ref, insem.at[4]),
    ]
    barrier = pltpu.get_barrier_semaphore()
    diagonal = [((gx + i) % DX, (gy + j) % DY) for i in (1, DX - 1) for j in (1, DY - 1)]
    known = [((gx + d) % DX, gy) for d in (1, DX - 1, 3, DX - 3, 8)] + [(gx, (gy + d) % DY) for d in (1, DY - 1, 3, DY - 3, 8)]
    for who in diagonal + known:
        pl.semaphore_signal(barrier, inc=1, device_id=who, device_id_type=MESH)
    for copy in inputs:
        copy.start()
    pl.semaphore_wait(barrier, len(diagonal) + len(known))

    copies = []
    n = 0
    for dx, dy in ((-1, -1), (-1, 1), (1, -1), (1, 1), (-1, 0), (1, 0), (0, -1), (0, 1)):
        wx = HX if dy == 0 else HX - 1
        sx = {1: (TX - wx, wx), -1: (0, wx), 0: (0, TX)}[dx]
        sy = {1: (TY - 4, 4), -1: (0, 4), 0: (0, TY)}[dy]
        tx = {1: HX - wx, -1: HX + TX, 0: HX}[dx]
        ty = {1: HY - 4, -1: HY + TY, 0: HY}[dy]
        copies.append(
            pltpu.make_async_remote_copy(
                src_ref=facies_hbm.at[pl.ds(sx[0], sx[1]), pl.ds(sy[0], sy[1])],
                dst_ref=fac.at[pl.ds(tx, sx[1]), pl.ds(ty, sy[1])],
                send_sem=hsend.at[n],
                recv_sem=hrecv.at[n],
                device_id=((gx + dx + DX) % DX, (gy + dy + DY) % DY),
                device_id_type=MESH,
            )
        )
        n += 1
    for copy in copies:
        copy.start()
    for who in known:
        pl.semaphore_signal(news, inc=1, device_id=who, device_id_type=MESH)

    for copy in inputs[1:]:
        copy.wait()
    well_x = wx_ref[...]
    well_y = wy_ref[...]
    well_r = wr_ref[...]
    sub64 = lax.broadcasted_iota(jnp.int32, (8, WELLS), 0)
    for j in range(2):
        hit_y = jnp.where(sub64 + (ay + 8 * j) == well_y, well_r, 0.0)
        for x in range(TX):
            part = jnp.where(well_x == ax + x, hit_y, 0.0)
            column = jnp.sum(part, axis=1, keepdims=True)
            rhs[x, 8 * j : 8 * j + 8, :] = source_ref[x, 8 * j : 8 * j + 8, :] + column / CELLS_Z

    last_z = flag(lane < CELLS_Z - 1)
    row_at = [ay - HY + 4 + 8 * t + sub for t in range(3)]
    row_m = [flag(inside(row - 1, GRID_Y) & inside(row, GRID_Y)) for row in row_at]
    row_p = [flag(inside(row, GRID_Y) & inside(row + 1, GRID_Y)) for row in row_at]
    same_ym = [[same_xy(row - 1, p, BLOCK_Y) for p in range(2)] for row in row_at]
    same_yp = [[same_xy(row, p, BLOCK_Y) for p in range(2)] for row in row_at]
    same_zm = [same_z(lane - 1, p) for p in range(2)]
    same_zp = [same_z(lane, p) for p in range(2)]

    def start_plane(x, _):
        gxe = ax - HX + x
        for t in range(4):
            row = ay - HY + 8 * t + sub
            for c, (i, j, k) in enumerate(COLORS):
                hit = inside(row, GRID_Y) & ((row // BLOCK_Y) % 2 == j) & ((lane // BLOCK_Z) % 2 == k)
                hitx = inside(gxe, GRID_X) & ((gxe + 2 * BLOCK_X) // BLOCK_X % 2 == i)
                va[c, x, 8 * t : 8 * t + 8, :] = flag(hit) * flag(hitx)
        return 0

    lax.fori_loop(0, EX, start_plane, 0)

    inputs[0].wait()

    half_inv = [0.5 / jnp.full((8, 128), perm_ref[f], F32) for f in range(FACIES)]
    store_at = [jnp.full((8, 128), store_ref[f], F32) for f in range(FACIES)]

    def pick(code, table):
        bits = [(code // (1 << b)) % 2 == 1 for b in range(3)]
        for b in range(3):
            table = [jnp.where(bits[b], hi, lo) for lo, hi in zip(table[::2], table[1::2])]
        return table[0]

    def lookup(tiles):
        def plane(x, _):
            for t in tiles:
                code = fac[x, 8 * t : 8 * t + 8, :]
                hperm[x, 8 * t : 8 * t + 8, :] = pick(code, half_inv)
                stor[x, 8 * t : 8 * t + 8, :] = pick(code, store_at)
            return 0

        return plane

    lax.fori_loop(HX, HX + TX, lookup((1, 2)), 0, unroll=2)

    def coefficients(tiles, *spans):
        def coef_plane(x, _):
            gxe = ax - HX + x
            ok_m = flag(inside(gxe - 1, GRID_X) & inside(gxe, GRID_X))
            ok_p = flag(inside(gxe, GRID_X) & inside(gxe + 1, GRID_X))
            for t in tiles:
                r = 4 + 8 * t
                h = hperm[x, r : r + 8, :]
                txm = ok_m / (h + hperm[x - 1, r : r + 8, :])
                txp = ok_p / (h + hperm[x + 1, r : r + 8, :])
                tym = row_m[t] / (h + hperm[x, r - 1 : r + 7, :])
                typ = row_p[t] / (h + hperm[x, r + 1 : r + 9, :])
                tzp = last_z / (h + roll(h, -1))
                tzm = roll(tzp, 1)
                diag = stor[x, r : r + 8, :] + txm + txp + tym + typ + tzm + tzp
                w = RELAX / diag
                wdiag[x, r : r + 8, :] = w
                for n, value in enumerate((txm, txp, tym, typ, tzm, tzp)):
                    trans[n, x, r : r + 8, :] = value
                wxm, wxp, wym, wyp, wzm, wzp = [w * v for v in (txm, txp, tym, typ, tzm, tzp)]
                a = 8 * t
                for p in range(2):
                    coef[p, x, a : a + 8, :] = wxm * same_xy(gxe - 1, p, BLOCK_X)
                    coef[2 + p, x, a : a + 8, :] = wxp * same_xy(gxe, p, BLOCK_X)
                    coef[4 + p, x, a : a + 8, :] = wym * same_ym[t][p]
                    coef[6 + p, x, a : a + 8, :] = wyp * same_yp[t][p]
                    coef[8 + p, x, a : a + 8, :] = wzm * same_zm[p]
                    coef[10 + p, x, a : a + 8, :] = wzp * same_zp[p]
            return 0

        for span in spans:
            lax.fori_loop(*span, coef_plane, 0, unroll=UNROLL_COEF)

    def sweep(src, dst, *spans, tiles=(0, 1, 2)):
        def plane(x, _):
            for t in tiles:
                r, a = 4 + 8 * t, 8 * t
                k = [coef[n, x, a : a + 8, :] for n in range(12)]
                old, new = [], []
                for c, (px, py, pz) in enumerate(COLORS):
                    v = src[c, x, r : r + 8, :]
                    q = k[px] * src[c, x - 1, r : r + 8, :] + k[2 + px] * src[c, x + 1, r : r + 8, :]
                    q += k[4 + py] * src[c, x, r - 1 : r + 7, :] + k[6 + py] * src[c, x, r + 1 : r + 9, :]
                    q += k[8 + pz] * roll(v, 1) + k[10 + pz] * roll(v, -1)
                    old.append(v)
                    new.append(q)
                total = functools.reduce(jnp.add, new) - RELAX * functools.reduce(jnp.add, old)
                keep = (1.0 - RELAX) - total
                for c in range(8):
                    dst[c, x, r : r + 8, :] = new[c] + old[c] * keep
            return 0

        for span in spans:
            lax.fori_loop(*span, plane, 0, unroll=UNROLL_SWEEP)

    inner, outer = (5, 11), ((1, 5), (11, 15))
    coefficients((1,), inner)
    sweep(va, vb, inner, tiles=(1,))
    for copy in copies[6:]:
        copy.wait_recv()
    lax.fori_loop(HX, HX + TX, lookup((0, 3)), 0, unroll=True)
    coefficients((0, 2), inner)
    sweep(va, vb, inner, tiles=(0, 2))
    sweep(vb, va, (6, 10))
    sweep(va, vb, (7, 9))
    for copy in copies[4:6]:
        copy.wait_recv()
    for span in ((0, HX), (HX + TX, EX)):
        lax.fori_loop(*span, lookup((1, 2)), 0, unroll=True)
    coefficients((1,), *outer)
    sweep(va, vb, *outer, tiles=(1,))
    for copy in copies[:4]:
        copy.wait_recv()
    for span in ((0, HX), (HX + TX, EX)):
        lax.fori_loop(*span, lookup((0, 3)), 0, unroll=True)
    coefficients((0, 2), *outer)
    sweep(va, vb, *outer, tiles=(0, 2))
    sweep(vb, va, (2, 6), (10, 14))
    sweep(va, vb, (3, 7), (9, 13))
    basis = vb

    tile_rows = [ay + 8 * t + sub for t in range(2)]
    tile_ym = [[same_xy(row - 1, p, BLOCK_Y) for p in range(2)] for row in tile_rows]
    tile_yp = [[same_xy(row, p, BLOCK_Y) for p in range(2)] for row in tile_rows]

    def apply_plane(x, _):
        for t in range(2):
            r = HY + 8 * t
            k = [trans[n, x, r : r + 8, :] for n in range(6)]
            s = stor[x, r : r + 8, :]
            ym, yp, zm, zp = tile_ym[t], tile_yp[t], same_zm, same_zp
            for c, (px, py, pz) in enumerate(COLORS):
                v = basis[c, x, r : r + 8, :]
                q = s * v
                q += k[0] * (v - basis[c, x - 1, r : r + 8, :]) + k[1] * (v - basis[c, x + 1, r : r + 8, :])
                q += k[2] * (v - ym[py] * basis[c, x, r - 1 : r + 7, :])
                q += k[3] * (v - yp[py] * basis[c, x, r + 1 : r + 9, :])
                q += k[4] * (v - zm[pz] * roll(v, 1)) + k[5] * (v - zp[pz] * roll(v, -1))
                bv[c, x - HX, 8 * t : 8 * t + 8, :] = q
                rimy[c, x - HX, 8 * t : 8 * t + 8, :] = (
                    (ym[1 - py] - 1.0) * k[2] * basis[c, x, r - 1 : r + 7, :]
                    + (yp[1 - py] - 1.0) * k[3] * basis[c, x, r + 1 : r + 9, :]
                )
        return 0

    lax.fori_loop(HX, HX + TX, apply_plane, 0, unroll=True)

    west = lane < 64
    cut_lo = [1.0 - same_z(lane, p) for p in range(2)]
    cut_hi = [1.0 - same_z(lane - 1, p) for p in range(2)]
    turn = lane % 32 >= 16

    def rim_plane(x, acc):
        acc = list(acc)
        for t in range(2):
            r = HY + 8 * t
            tzm, tzp = trans[4, x, r : r + 8, :], trans[5, x, r : r + 8, :]
            lo = [-tzp * cut_lo[1 - p] for p in range(2)]
            hi = [-tzm * cut_hi[1 - p] for p in range(2)]
            both = -tzp * (cut_lo[0] + cut_lo[1])
            vs = [basis[c, x, r : r + 8, :] for c in range(8)]
            up = [roll(v, -1) for v in vs]
            for c, (px, py, pz) in enumerate(COLORS):
                rim[c, x - HX, 8 * t : 8 * t + 8, :] = lo[pz] * up[c] + hi[pz] * roll(vs[c], 1)
            here = [jnp.where(turn, vs[c], vs[c + 2]) for c in (0, 1, 4, 5)]
            there = [jnp.where(turn, up[c], up[c + 2]) for c in (0, 1, 4, 5)]
            first = [both * jnp.where(west, a, b) for a, b in zip(here, there)]
            second = [jnp.where(west, b, a) for a, b in zip(here, there)]
            for m in range(4):
                for n in range(4):
                    acc[4 * m + n] = acc[4 * m + n] + first[m] * second[n]
        return tuple(acc)

    zeros16 = tuple(jnp.zeros((8, 128), F32) for _ in range(16))
    acc = lax.fori_loop(HX, HX + TX, rim_plane, zeros16, unroll=True)
    for n in range(8, 12):
        wide[n] = jnp.zeros((8, 128), F32)
    corner4, edge4 = (0, 1, 4, 5), (2, 3, 6, 7)
    for m in range(4):
        for n in range(4):
            wide[8 + m, corner4[n] : corner4[n] + 1, :] = jnp.sum(acc[4 * m + n], axis=0, keepdims=True)

    parity_y = jnp.where(gy == 9, 1, 0)
    at_rim = jnp.where((gy == 5) | (gy == 9), -1.0, 0.0).astype(F32)
    top = flag(sub == 7) * at_rim

    def rim_y_plane(x, acc):
        acc = list(acc)
        t = trans[3, x, HY + 8 : HY + 16, :] * top
        here = [t * basis[c + parity_y, x, HY + 8 : HY + 16, :] for c in (0, 2, 4, 6)]
        there = [basis[c + parity_y, x, HY + 9 : HY + 17, :] for c in (0, 2, 4, 6)]
        for m in range(4):
            for n in range(4):
                acc[4 * m + n] = acc[4 * m + n] + here[m] * there[n]
        return tuple(acc)

    acc = lax.fori_loop(HX, HX + TX, rim_y_plane, zeros16, unroll=True)
    for m in range(4):
        for n in range(4):
            line = jnp.sum(acc[4 * m + n], axis=0, keepdims=True)
            wide[12 + m, 2 * n : 2 * n + 1, :] = line
            wide[12 + n, 2 * m + 1 : 2 * m + 2, :] = line

    pairs = [(a, c) for a in range(8) for c in range(a, 8)]
    for group in (pairs[:15], pairs[15:30], pairs[30:]):
        rows = sorted({a for a, _ in group})
        cols = sorted({c for _, c in group})
        last = group[-1] == (7, 7)

        def gather(x, acc, group=group, rows=rows, cols=cols, last=last):
            acc = list(acc)
            for t in range(2):
                r = HY + 8 * t
                at = slice(8 * t, 8 * t + 8)
                left = {a: basis[a, x + HX, r : r + 8, :] for a in (range(8) if last else rows)}
                right = {c: bv[c, x, at, :] for c in cols}
                own = {c: basis[c, x + HX, r : r + 8, :] for c in cols}
                over_z = {a: rim[a, x, at, :] for a in rows}
                over_y = {a: rimy[a, x, at, :] for a in rows}
                for n, (a, c) in enumerate(group):
                    acc[n] = acc[n] + left[a] * right[c]
                    if COLORS[a][2] != COLORS[c][2] and COLORS[a][1] != COLORS[c][1]:
                        acc[n] = acc[n] + own[c] * (over_z[a] + over_y[a])
                    elif COLORS[a][2] != COLORS[c][2]:
                        acc[n] = acc[n] + own[c] * over_z[a]
                    elif COLORS[a][1] != COLORS[c][1]:
                        acc[n] = acc[n] + own[c] * over_y[a]
                if last:
                    load = rhs[x, at, :]
                    for a in range(8):
                        acc[len(group) + a] = acc[len(group) + a] + left[a] * load
            return tuple(acc)

        count = len(group) + (8 if last else 0)
        acc = lax.fori_loop(0, TX, gather, tuple(jnp.zeros((8, 128), F32) for _ in range(count)), unroll=True)
        for n, (a, c) in enumerate(group):
            line = jnp.sum(acc[n], axis=0, keepdims=True)
            wide[c, a : a + 1, :] = line
            if a != c:
                wide[a, c : c + 1, :] = line
        if last:
            for a in range(8):
                at = (8, a) if a in edge4 else (9, a + 2)
                wide[at[0], at[1] : at[1] + 1, :] = jnp.sum(acc[len(group) + a], axis=0, keepdims=True)

    def ranges(places):
        total = jnp.zeros((8, 128), F32)
        for n, slot in places:
            line = wide[n]
            for step in (1, 2, 4, 8):
                line = line + roll(line, -step)
            line = jnp.where(lane % 16 == 8, line, 0.0)
            total = total + roll(line, 8 + slot)
        return total

    mine[...] = ranges(
        [(n, n) for n in range(8)] + [(8 + m, 8 + corner4[m]) for m in range(4)] + [(12 + m, 8 + edge4[m]) for m in range(4)]
    )
    pl.semaphore_wait(news, len(known))

    def exchange(src, slots, send, recv, axis, earlier):
        me = gx if axis == 0 else gy
        size = DX if axis == 0 else DY
        for d in range(1, size):
            to = ((gx + d) % DX, gy) if axis == 0 else (gx, (gy + d) % DY)
            pltpu.make_async_remote_copy(
                src_ref=src, dst_ref=slots.at[me], send_sem=send, recv_sem=recv,
                device_id=to, device_id_type=MESH,
            ).start()
        slots[me] = src[...]
        for copy in earlier:
            copy.wait_send() if axis == 0 else copy.wait()
        arrived = slots.at[pl.ds(0, size - 1)]
        pltpu.make_async_copy(arrived, arrived, recv).wait()
        return pltpu.make_async_copy(arrived, arrived, send)

    def tree(items):
        while len(items) > 1:
            items = [a + b for a, b in zip(items[::2], items[1::2])] + (items[-1:] if len(items) % 2 else [])
        return items[0]

    sent_x = exchange(mine, stage1, xsend, xrecv, 0, copies)
    half[...] = tree([stage1[n] for n in range(DX)])
    sent_y = exchange(half, stage2, ysend, yrecv, 1, [sent_x])

    pa, pb, pc = [tree([stage2[n] for n in range(*ends)]) for ends in ((0, 6), (6, 10), (10, 16))]
    slot = lane % 16
    ly, sy = lane % 2, sub % 2
    lk, sk = lane // 2 % 2, sub // 2 % 2

    def keep(cond, value):
        return jnp.where(cond, value, 0.0)

    def rows_up(value, shift):
        return pltpu.roll(value, shift % 8, 0)

    m00, m01 = (ly == 0) & (sy == 0), (ly == 0) & (sy == 1)
    m10, m11 = (ly == 1) & (sy == 0), (ly == 1) & (sy == 1)
    qa, qb = [keep(slot % 4 == 0, roll(p, -10)) + keep(slot % 4 == 2, roll(p, -9)) for p in (pa, pb)]
    pairs_y = slot < 8
    y01 = keep(pairs_y & m00, qa) + keep(pairs_y & m11, rows_up(roll(qb, 1), 1))
    y10 = keep(pairs_y & m00, rows_up(qa, -1)) + keep(pairs_y & m11, roll(qb, 1))
    joined = [[pa + keep(m11, pb), keep(m10, pb) + y01], [keep(m01, pb) + y10, pc + keep(m00, pb)]]
    by_row = []
    for pk in range(2):
        picked = [[keep(lk == pk, joined[h][g]) for g in range(2)] for h in range(2)]
        by_row.append([
            (picked[0][g] + roll(picked[1][g], 2)) if pk == 0 else (roll(picked[0][g], -2) + picked[1][g])
            for g in range(2)
        ])

    def by_column(values, pk):
        low, high = keep(sk == pk, values[0]), keep(sk == pk, values[1])
        return low + rows_up(high, 2) if pk == 0 else rows_up(low, -2) + high

    node = [[by_column(by_row[pk], pq) for pq in range(2)] for pk in range(2)]
    loads = [pa + keep(sy == 1, pb), pc + keep(sy == 0, pb)]
    load_of = [
        keep(sk == 0, rows_up(roll(loads[0], -8), -2)) + keep(sk == 1, roll(loads[1], -8)),
        rows_up(keep(sk == 1, roll(loads[0], -7)), -2) + keep(sk == 1, roll(loads[1], -7)),
    ]
    layer = lane // 16
    even = layer % 2 == 0
    own = jnp.where(even, node[0][0] + roll(node[0][0], -16), node[1][1] + roll(node[1][1], -16))
    near_k = jnp.where(even, node[0][1], node[1][0])
    near_up = jnp.where(even, roll(node[0][1], -16), roll(node[1][0], -16))
    near_k = jnp.where(layer < 4, near_up, near_k)
    far_k = jnp.where(layer < 4, roll(node[0][0], -24), roll(node[0][0], 8))
    load_k = jnp.where(even, load_of[0] + roll(load_of[0], -16), load_of[1] + roll(load_of[1], -16))

    def ends(value, level, at):
        a, b = 16 * level + at, 16 * (7 - level) + at
        return jnp.where(west, jnp.broadcast_to(value[:, a : a + 1], (8, 128)), jnp.broadcast_to(value[:, b : b + 1], (8, 128)))

    def all_lanes(value, at):
        return jnp.broadcast_to(value[:, at : at + 1], (8, 128))

    def spread(value, k):
        return jnp.broadcast_to(value[k : k + 1, :], (8, 128))

    def eliminate(block, nexts, load, after):
        block, nexts = list(block), [list(b) for b in nexts]
        load = [spread(load, k) for k in range(8)]
        for k in range(8):
            inverse = 1.0 / spread(block[k], k)
            pivot = block[k] * inverse
            scaled = [b[k] * inverse for b in nexts]
            scaled_load = load[k] * inverse
            after([b[k] for b in nexts], scaled, scaled_load)
            for i in range(8):
                if i == k:
                    continue
                f = spread(block[i], k)
                block[i] = block[i] - f * pivot
                for b, v in zip(nexts, scaled):
                    b[i] = b[i] - f * v
                load[i] = load[i] - f * scaled_load
            block[k] = pivot
            for b, v in zip(nexts, scaled):
                b[k] = v
            load[k] = scaled_load
        return nexts, load

    diag = [[ends(own, l, i) for i in range(8)] for l in range(3)]
    one = [[ends(near_k, l, i) for i in range(8)] for l in range(3)]
    two = [[ends(far_k, l, i) for i in range(8)] for l in range(3)]
    right = [ends(load_k, l, 1) for l in range(3)]
    zero = jnp.zeros((8, 128), F32)
    d3, d4, d34 = [zero] * 8, [zero] * 8, [zero] * 8
    r3, r4 = zero, zero
    solved = []
    for level in range(3):
        def after(raw, scaled, load, level=level):
            nonlocal r3, r4
            p1, p2 = raw
            s1, s2 = scaled
            for i in range(8):
                f1, f2 = spread(p1, i), spread(p2, i)
                if level == 0:
                    diag[1][i] = diag[1][i] - f1 * s1
                    one[1][i] = one[1][i] - f1 * s2
                    diag[2][i] = diag[2][i] - f2 * s2
                elif level == 1:
                    diag[2][i] = diag[2][i] - f1 * s1
                    one[2][i] = one[2][i] - f1 * s2
                    d3[i] = d3[i] - f2 * s2
                else:
                    d3[i] = d3[i] - f1 * s1
                    d4[i] = d4[i] - f2 * s2
                    d34[i] = d34[i] - jnp.where(west, f1, f2) * jnp.where(west, s2, s1)
            if level == 0:
                right[1] = right[1] - p1 * load
                right[2] = right[2] - p2 * load
            elif level == 1:
                right[2] = right[2] - p1 * load
                r3 = r3 - p2 * load
            else:
                r3 = r3 - p1 * load
                r4 = r4 - p2 * load

        solved.append(eliminate(diag[level], [one[level], two[level]], right[level], after))

    def meet(a, b):
        value = jnp.where(west, a, b)
        return value + roll(value, 64)

    m3 = [all_lanes(own, 48 + i) + meet(d3[i], d4[i]) for i in range(8)]
    m4 = [all_lanes(own, 64 + i) + meet(d4[i], d3[i]) for i in range(8)]
    m34 = [all_lanes(near_k, 48 + i) + d34[i] + roll(d34[i], 64) for i in range(8)]
    v3 = all_lanes(load_k, 49) + meet(r3, r4)
    v4 = all_lanes(load_k, 65) + meet(r4, r3)

    def after_three(raw, scaled, load):
        nonlocal v4
        for i in range(8):
            m4[i] = m4[i] - spread(raw[0], i) * scaled[0]
        v4 = v4 - raw[0] * load

    (up3,), load3 = eliminate(m3, [m34], v3, after_three)
    _, x4 = eliminate(m4, [], v4, lambda *_: None)

    def column(items):
        value = items[0]
        for i in range(1, 8):
            value = jnp.where(sub == i, items[i], value)
        return value

    def total(value):
        return jnp.broadcast_to(jnp.sum(value, axis=0, keepdims=True), (8, 128))

    c4 = column(x4)
    x3 = [load3[i] - total(up3[i] * c4) for i in range(8)]
    c3 = column(x3)
    first, second = jnp.where(west, c3, c4), jnp.where(west, c4, c3)
    x_of = [None] * 3
    for level in (2, 1, 0):
        (n1, n2), load = solved[level]
        x_of[level] = [load[i] - total(n1[i] * first + n2[i] * second) for i in range(8)]
        first, second = column(x_of[level]), first

    node_k = [2 * ((lane + BLOCK_Z // 2) // (2 * BLOCK_Z)),
              2 * ((lane + BLOCK_Z // 2 + BLOCK_Z) // (2 * BLOCK_Z)) - 1]
    for p in range(2):
        k = node_k[p]
        at = [((k == level) & west) | ((k == 7 - level) & ~west) for level in range(3)]
        for ij in range(8):
            line = keep(k == 3, x3[ij]) + keep(k == 4, x4[ij])
            for level in range(3):
                line = jnp.where(at[level], x_of[level][ij], line)
            val[p, ij : ij + 1, :] = line[0:1, :]

    def node_row(px, py, pz, tile):
        first = tile * TY
        j = py + 2 * ((first + BLOCK_Y // 2 - BLOCK_Y * py + 4 * BLOCK_Y) // (2 * BLOCK_Y) - 2)
        j = jnp.clip(j, 0, 3)
        return val[pz, pl.ds(4 * px + j, 1), :]

    before, here, beyond = [[node_row(px, py, pz, gy + d) for px, py, pz in COLORS] for d in (-1, 0, 1)]
    for t in range(3):
        r = HY - 1 + 8 * t
        first, others = ((before, here), (here, here), (here, beyond))[t]
        weights = [jnp.where(sub == 0, a, b) for a, b in zip(first, others)]

        def prolong(x, _, r=r, weights=weights):
            prol[x, r : r + 8, :] = functools.reduce(
                jnp.add, [weights[c] * basis[c, x, r : r + 8, :] for c in range(8)]
            )
            return 0

        lax.fori_loop(HX - 1, HX + TX + 1, prolong, 0, unroll=5)


    def finish(x, _):
        for t in range(2):
            r = HY + 8 * t
            v = prol[x, r : r + 8, :]
            k = [trans[n, x, r : r + 8, :] for n in range(6)]
            q = stor[x, r : r + 8, :] * v
            q += k[0] * (v - prol[x - 1, r : r + 8, :]) + k[1] * (v - prol[x + 1, r : r + 8, :])
            q += k[2] * (v - prol[x, r - 1 : r + 7, :]) + k[3] * (v - prol[x, r + 1 : r + 9, :])
            q += k[4] * (v - roll(v, 1)) + k[5] * (v - roll(v, -1))
            load = rhs[x - HX, 8 * t : 8 * t + 8, :]
            out_ref[x - HX, 8 * t : 8 * t + 8, :] = v + wdiag[x, r : r + 8, :] * (load - q)
        return 0

    lax.fori_loop(HX, HX + TX, finish, 0, unroll=True)
    sent_y.wait()


def per_device(facies, source, facies_perm, facies_store, well_x, well_y, well_rate):
    vmem = pl.BlockSpec(memory_space=pltpu.VMEM)
    smem = pl.BlockSpec(memory_space=pltpu.SMEM)
    hbm = pl.BlockSpec(memory_space=pltpu.HBM)
    field = pltpu.VMEM((EX, EY, 128), F32)
    colors = pltpu.VMEM((8, EX, EY, 128), F32)
    return pl.pallas_call(
        kernel,
        out_shape=jax.ShapeDtypeStruct((TX, TY, CELLS_Z), F32),
        in_specs=[hbm, hbm, smem, smem, hbm, hbm, hbm],
        out_specs=vmem,
        scratch_shapes=[
            pltpu.VMEM((EX, EY, 128), jnp.int32),
            field,
            field,
            pltpu.VMEM((12, EX, 24, 128), F32),
            pltpu.VMEM((6, EX, EY, 128), F32),
            field,
            colors,
            colors,
            pltpu.VMEM((8, TX, TY, 128), F32),
            pltpu.VMEM((8, TX, TY, 128), F32),
            pltpu.VMEM((8, TX, TY, 128), F32),
            pltpu.VMEM((TX, TY, 128), F32),
            pltpu.VMEM((16, 8, 128), F32),
            pltpu.VMEM((DX, 8, 128), F32),
            pltpu.VMEM((DY, 8, 128), F32),
            pltpu.VMEM((2, 8, 128), F32),
            field,
            pltpu.VMEM((8, 128), F32),
            pltpu.VMEM((8, 128), F32),
            pltpu.VMEM((TX, TY, 128), F32),
            pltpu.VMEM((1, WELLS), jnp.int32),
            pltpu.VMEM((1, WELLS), jnp.int32),
            pltpu.VMEM((1, WELLS), F32),
            pltpu.SemaphoreType.DMA((5,)),
            pltpu.SemaphoreType.DMA((8,)),
            pltpu.SemaphoreType.DMA((8,)),
            pltpu.SemaphoreType.DMA,
            pltpu.SemaphoreType.DMA,
            pltpu.SemaphoreType.DMA,
            pltpu.SemaphoreType.DMA,
            pltpu.SemaphoreType.REGULAR,
        ],
        compiler_params=pltpu.CompilerParams(
            collective_id=0, has_side_effects=True, vmem_limit_bytes=40 * 1024 * 1024
        ),
    )(
        facies, source, facies_perm, facies_store,
        well_x.reshape(1, WELLS), well_y.reshape(1, WELLS), well_rate.reshape(1, WELLS),
    )


def solution(mesh):
    in_specs = (P("gx", "gy", None), P("gx", "gy", None), P(), P(), P(), P(), P())
    return jax.shard_map(
        per_device, mesh=mesh, in_specs=in_specs, out_specs=P("gx", "gy", None), check_vma=False
    )
```
